128 devices in a mesh: grid: 32 (over x, y, core), mesh: 4 (over z).
Axes of the slice: x: 4, y: 4, z: 4, core: 2. Of those that a mesh axis runs over, the one named last changes fastest.
Arguments:
- grid_latent: bfloat16 [131072, 512], P(('grid', 'mesh')), may hold values from -6 to 6
- mesh_latent: bfloat16 [20480, 512], P(('grid', 'mesh')), may hold values from -6 to 6
- enc_source: int32 [262144], P(('grid', 'mesh')), may hold values from 0 to 1023
- enc_slot: int32 [262144], P(('grid', 'mesh')), may hold values from 0 to 1023, as said below
- enc_geometry: float32 [4, 262144], P(None, ('grid', 'mesh')), may hold values from -6 to 6
- edge_count: int32 [128], P(('grid', 'mesh')), may hold values from 512 to 2048, as said below
- slot_row: int32 [128, 2, 4, 128], P(('grid', 'mesh')), may hold values from 0 to 159
- halo_rows: int32 [128, 128, 8], P(('grid', 'mesh')), may hold values from 0 to 159
- proc_source: int32 [163840], P(('grid', 'mesh')), may hold values from 0 to 1183
- proc_target: int32 [163840], P(('grid', 'mesh')), may hold values from 0 to 159
- proc_geometry: float32 [4, 163840], P(None, ('grid', 'mesh')), may hold values from -6 to 6
- return_rows: int32 [128, 2, 4, 128], P(('grid', 'mesh')), may hold values from 0 to 159
- dec_source: int32 [131072, 3], P(('grid', 'mesh')), may hold values from 0 to 1023, as said below
- dec_geometry: float32 [4, 3, 131072], P(None, None, ('grid', 'mesh')), may hold values from -6 to 6
- enc_weights: bfloat16 [5, 512, 512], replicated, may hold values from -0.25 to 0.25
- enc_lift: float32 [4, 512], replicated, may hold values from -3 to 3
- proc_weights: bfloat16 [2, 6, 512, 512], replicated, may hold values from -0.25 to 0.25
- proc_lift: float32 [2, 4, 512], replicated, may hold values from -3 to 3
- dec_weights: bfloat16 [3, 512, 512], replicated, may hold values from -0.25 to 0.25
- dec_lift: float32 [4, 512], replicated, may hold values from -3 to 3
Outputs:
- grid_out: bfloat16 [131072, 512], P(('grid', 'mesh'))
- mesh_out: bfloat16 [20480, 512], P(('grid', 'mesh'))
The draws below stay inside these ranges and needn't reach their ends.
Inputs may be any that keep to these rules, and one draw needn't show every extreme that they name: An edge of a device in strip g feeds strip g + enc_slot // (4 * 128), one of its own strip and the next (2 strips); devices of the last strip use only their own strip. `edge_count`: some device has all 2048 edges live. A grid node of strip g reads from strip g + dec_source // (4 * 128), its own or the next; nodes of the last strip read only from their own strip.
All inputs are finite; a program needn't handle non-finite values.
Results may differ from the reference program's by a relative error of at most 0.02.
Values may be sent and summed in bfloat16 or wider, within the bound.
No kernel may reach another device: no remote copies, remote signals or barrier semaphores. Data moves between devices by JAX's collectives and lax.ppermute only.
A program may use at most 64 MiB of HBM per device.

```python
import jax
import jax.numpy as jnp
from jax import lax

LAT = 512
G_DEV = 1024
M_DEV = 160
LAYERS = 2
NEAR = 3
BAND_G = 2
CAP = 128
HB = 8
RB = 128
SHARDS = 128
E1_DEV = 2048
ME_DEV = 1280
G_TOTAL = 131072
M_TOTAL = 20480
E1_TOTAL = 262144
ME_TOTAL = 163840
N_GRID = 32
N_MESH = 4


def draw_edge_count(key, part):
    key = jax.random.fold_in(key, 7)
    first, second = jax.random.split(key)
    counts = jax.random.randint(first, (SHARDS,), E1_DEV // 4, E1_DEV + 1)
    fullest = jax.random.randint(second, (), 0, SHARDS)
    return counts.at[fullest].set(E1_DEV).astype(jnp.int32)


def banded(key, rows, per_device, block):
    device = jnp.arange(rows, dtype=jnp.int32) // per_device
    strip = device // N_MESH
    upper = jnp.where(strip == N_GRID - 1, N_MESH * block, BAND_G * N_MESH * block).astype(jnp.int32)
    unit = jax.random.randint(key, (rows,), 0, BAND_G * N_MESH * block * 64)
    return (unit % upper).astype(jnp.int32)


def draw_enc_slot(key, part):
    key = jax.random.fold_in(key, 11)
    return banded(key, E1_TOTAL, E1_DEV, CAP)


def draw_dec_source(key, part):
    key = jax.random.fold_in(key, 13)
    flat = banded(key, G_TOTAL * NEAR, G_DEV * NEAR, RB)
    return flat.reshape(G_TOTAL, NEAR)


def with_ends(array, stream_key, smallest, top_value):
    spot = [jax.random.randint(jax.random.fold_in(stream_key, axis), (), 0, length) for axis, length in enumerate(array.shape)]
    longest = array.shape.index(max(array.shape))
    beside = spot[:longest] + [(spot[longest] + 1) % array.shape[longest]] + spot[longest + 1:]
    return array.at[tuple(spot)].set(smallest).at[tuple(beside)].set(top_value)


def block_levels(key, dims, cuts, low, top_value):
    def one(axis_at, parts):
        draws = jax.random.uniform(jax.random.fold_in(jax.random.fold_in(key, 6), axis_at), (parts,), jnp.float32, low / len(cuts), top_value / len(cuts))
        return jnp.repeat(jnp.exp(draws), dims[axis_at] // parts).reshape((-1,) + (1,) * (len(dims) - axis_at - 1))

    loudness = one(*cuts[0])
    for cut in cuts[1:]:
        loudness = loudness * one(*cut)
    return loudness


def normal_values(own_key, extent, deviation, bound, shards=(), held_as=jnp.bfloat16):
    values = jax.random.normal(own_key, extent, jnp.float32) * deviation
    if len(shards) > 0:
        values = block_levels(own_key, extent, shards, -0.22, 0.18) * values
    return jnp.clip(values, min=-bound, max=bound).astype(held_as)


def setup_inputs(seed: int = 0) -> dict:
    arg_keys = jax.random.split(jax.random.key(seed), 21)
    return {
        "grid_latent": normal_values(arg_keys[0], (G_TOTAL, LAT), 1.0, 6.0, ((0, 128),)),
        "mesh_latent": normal_values(arg_keys[1], (M_TOTAL, LAT), 1.0, 6.0, ((0, 128),)),
        "enc_source": with_ends(jax.random.randint(arg_keys[2], (E1_TOTAL,), 0, G_DEV), jax.random.fold_in(arg_keys[2], 1), 0, G_DEV - 1).astype(jnp.int32),
        "enc_slot": draw_enc_slot(jax.random.fold_in(arg_keys[20], 71), 0),
        "enc_geometry": normal_values(arg_keys[4], (4, E1_TOTAL), 1.0, 6.0, ((1, 128),), jnp.float32),
        "edge_count": draw_edge_count(jax.random.fold_in(arg_keys[20], 71), 0),
        "slot_row": with_ends(jax.random.randint(arg_keys[6], (SHARDS, BAND_G, N_MESH, CAP), 0, M_DEV), jax.random.fold_in(arg_keys[6], 1), 0, M_DEV - 1).astype(jnp.int32),
        "halo_rows": with_ends(jax.random.randint(arg_keys[7], (SHARDS, SHARDS, HB), 0, M_DEV), jax.random.fold_in(arg_keys[7], 1), 0, M_DEV - 1).astype(jnp.int32),
        "proc_source": with_ends(jax.random.randint(arg_keys[8], (ME_TOTAL,), 0, M_DEV + SHARDS * HB), jax.random.fold_in(arg_keys[8], 1), 0, (M_DEV + SHARDS * HB) - 1).astype(jnp.int32),
        "proc_target": with_ends(jax.random.randint(arg_keys[9], (ME_TOTAL,), 0, M_DEV), jax.random.fold_in(arg_keys[9], 1), 0, M_DEV - 1).astype(jnp.int32),
        "proc_geometry": normal_values(arg_keys[10], (4, ME_TOTAL), 1.0, 6.0, ((1, 128),), jnp.float32),
        "return_rows": with_ends(jax.random.randint(arg_keys[11], (SHARDS, BAND_G, N_MESH, RB), 0, M_DEV), jax.random.fold_in(arg_keys[11], 1), 0, M_DEV - 1).astype(jnp.int32),
        "dec_source": draw_dec_source(jax.random.fold_in(arg_keys[20], 71), 0),
        "dec_geometry": normal_values(arg_keys[13], (4, NEAR, G_TOTAL), 1.0, 6.0, ((2, 128),), jnp.float32),
        "enc_weights": normal_values(arg_keys[14], (5, LAT, LAT), LAT ** -0.5, 0.25),
        "enc_lift": normal_values(arg_keys[15], (4, LAT), 4 ** -0.5, 3.0, (), jnp.float32),
        "proc_weights": normal_values(arg_keys[16], (LAYERS, 6, LAT, LAT), LAT ** -0.5, 0.25),
        "proc_lift": normal_values(arg_keys[17], (LAYERS, 4, LAT), 4 ** -0.5, 3.0, (), jnp.float32),
        "dec_weights": normal_values(arg_keys[18], (3, LAT, LAT), LAT ** -0.5, 0.25),
        "dec_lift": normal_values(arg_keys[19], (4, LAT), 4 ** -0.5, 3.0, (), jnp.float32),
    }


def layer_norm(values):
    centered = values - lax.optimization_barrier(jnp.mean(values, axis=-1, keepdims=True))
    spread = lax.optimization_barrier(jnp.mean(centered * centered, axis=-1, keepdims=True))
    return centered * lax.rsqrt(spread + 1e-05)

def lift(geometry, weight):
    return jnp.dot(geometry.T, weight, precision=lax.Precision.HIGHEST, preferred_element_type=jnp.float32)

def node_update(latent, total, w_self, w_total, w_out):
    inner = jnp.dot(latent, w_self, preferred_element_type=jnp.float32)
    inner = inner + jnp.dot(total.astype(jnp.bfloat16), w_total, preferred_element_type=jnp.float32)
    hidden = jax.nn.silu(inner).astype(jnp.bfloat16)
    update = layer_norm(jnp.dot(hidden, w_out, preferred_element_type=jnp.float32))
    return (latent.astype(jnp.float32) + update).astype(jnp.bfloat16)

def reference(grid_latent, mesh_latent, enc_source, enc_slot, enc_geometry, edge_count, slot_row, halo_rows, proc_source, proc_target, proc_geometry, return_rows, dec_source, dec_geometry, enc_weights, enc_lift, proc_weights, proc_lift, dec_weights, dec_lift):
    owners = jnp.arange(SHARDS, dtype=jnp.int32)
    slots = jnp.arange(BAND_G * N_MESH * CAP, dtype=jnp.int32)
    slot_offset = slots // (N_MESH * CAP)
    slot_mesh = slots // CAP % N_MESH
    slot_place = slots % CAP

    def encode(total, owner):
        strip = owner // N_MESH
        column = owner % N_MESH
        rows = lax.dynamic_slice_in_dim(grid_latent, owner * G_DEV, G_DEV, 0)
        source = lax.dynamic_slice_in_dim(enc_source, owner * E1_DEV, E1_DEV, 0)
        slot = lax.dynamic_slice_in_dim(enc_slot, owner * E1_DEV, E1_DEV, 0)
        geometry = lax.dynamic_slice_in_dim(enc_geometry, owner * E1_DEV, E1_DEV, 1)
        projected = jnp.dot(rows, enc_weights[0], preferred_element_type=jnp.float32)
        hidden = jax.nn.silu(projected[source] + lift(geometry, enc_lift)).astype(jnp.bfloat16)
        message = layer_norm(jnp.dot(hidden, enc_weights[1], preferred_element_type=jnp.float32))
        live = jnp.arange(E1_DEV, dtype=jnp.int32) < edge_count[owner]
        message = jnp.where(live[:, None], message, jnp.zeros_like(message))
        partial_value = jax.ops.segment_sum(message, slot, num_segments=BAND_G * N_MESH * CAP)
        receiver = jnp.minimum((strip + slot_offset) * N_MESH + slot_mesh, SHARDS - 1).astype(jnp.int32)
        target = receiver * M_DEV + slot_row[receiver, slot_offset, column, slot_place]
        return (total.at[target].add(partial_value), None)
    start = jnp.zeros((M_TOTAL, LAT), jnp.float32)
    enc_total, unused = lax.scan(encode, start, owners)
    latent = node_update(mesh_latent, enc_total, enc_weights[2], enc_weights[3], enc_weights[4])
    for layer in range(LAYERS):
        weights = proc_weights[layer]
        from_sender = jnp.dot(latent, weights[0], preferred_element_type=jnp.float32)
        at_target = jnp.dot(latent, weights[1], preferred_element_type=jnp.float32)
        lift_weight = proc_lift[layer]

        def process(owner):
            source = lax.dynamic_slice_in_dim(proc_source, owner * ME_DEV, ME_DEV, 0)
            target = lax.dynamic_slice_in_dim(proc_target, owner * ME_DEV, ME_DEV, 0)
            geometry = lax.dynamic_slice_in_dim(proc_geometry, owner * ME_DEV, ME_DEV, 1)
            remote = jnp.maximum(source - M_DEV, 0)
            peer = remote // HB
            place = remote % HB
            sender = jnp.where(source < M_DEV, owner * M_DEV + source, peer * M_DEV + halo_rows[peer, owner, place])
            preact = from_sender[sender] + at_target[owner * M_DEV + target] + lift(geometry, lift_weight)
            hidden = jax.nn.silu(preact).astype(jnp.bfloat16)
            message = layer_norm(jnp.dot(hidden, weights[2], preferred_element_type=jnp.float32))
            return jax.ops.segment_sum(message, target, num_segments=M_DEV)
        proc_total = lax.map(process, owners).reshape(M_TOTAL, LAT)
        latent = node_update(latent, proc_total, weights[3], weights[4], weights[5])
    mesh_out = latent
    dec_proj = jnp.dot(mesh_out, dec_weights[0], preferred_element_type=jnp.float32).astype(jnp.bfloat16)

    def decode(owner):
        strip = owner // N_MESH
        column = owner % N_MESH
        rows = lax.dynamic_slice_in_dim(grid_latent, owner * G_DEV, G_DEV, 0)
        chosen = lax.dynamic_slice_in_dim(dec_source, owner * G_DEV, G_DEV, 0)
        geometry = lax.dynamic_slice_in_dim(dec_geometry, owner * G_DEV, G_DEV, 2)
        offset = chosen // (N_MESH * RB)
        peer_mesh = chosen // RB % N_MESH
        place = chosen % RB
        peer = jnp.minimum((strip + offset) * N_MESH + peer_mesh, SHARDS - 1).astype(jnp.int32)
        node = peer * M_DEV + return_rows[peer, offset, column, place]
        own = jnp.dot(rows, dec_weights[1], preferred_element_type=jnp.float32)
        total = jnp.zeros((G_DEV, LAT), jnp.float32)
        for which in range(NEAR):
            preact = dec_proj[node[:, which]].astype(jnp.float32) + own + lift(geometry[:, which, :], dec_lift)
            hidden = jax.nn.silu(preact).astype(jnp.bfloat16)
            total = total + jnp.dot(hidden, dec_weights[2], preferred_element_type=jnp.float32)
        return (rows.astype(jnp.float32) + layer_norm(total)).astype(jnp.bfloat16)
    grid_out = lax.map(decode, owners).reshape(G_TOTAL, LAT)
    return (grid_out, mesh_out)
```

```python
import functools

import jax
import jax.numpy as jnp
from jax import lax
from jax.experimental import pallas as pl
from jax.experimental.pallas import tpu as pltpu
from jax.sharding import PartitionSpec as P

BF = jnp.bfloat16
F32 = jnp.float32
VM = pl.BlockSpec(memory_space=pltpu.VMEM)
SM = pl.BlockSpec(memory_space=pltpu.SMEM)
HB = pl.BlockSpec(memory_space=pltpu.HBM)
ANY = pl.BlockSpec(memory_space=pl.ANY)
MIB = 1024 * 1024
BLOCK = 256


def mm(a, b):
    return lax.dot_general(a, b, (((1,), (0,)), ((), ())), preferred_element_type=F32)


def mm_tn(a, b):
    return lax.dot_general(a, b, (((0,), (0,)), ((), ())), preferred_element_type=F32)


def to_columns(row):
    n = row.shape[1]
    parts = [jnp.broadcast_to(row[:, at:at + 128], (128, 128)).T for at in range(0, n, 128)]
    return jnp.concatenate(parts, axis=0) if len(parts) > 1 else parts[0]


def lane_hits(columns, at):
    return columns - jnp.int16(at) == lax.broadcasted_iota(jnp.int16, columns.shape, 1)


def as_ones(hits):
    return jnp.where(hits, jnp.ones(hits.shape, BF), jnp.zeros(hits.shape, BF))


def pick_matrix(columns, width):
    col = columns.astype(jnp.int16)
    return jnp.concatenate([as_ones(lane_hits(col, at)) for at in range(0, width, 128)], axis=1)


def add_matrix(row, height):
    n = row.shape[1]
    wide = jnp.broadcast_to(row, (16, n)).astype(jnp.int16)
    wide = jnp.broadcast_to(wide[None], (height // 16, 16, n)).reshape(height, n)
    return as_ones(wide == lax.broadcasted_iota(jnp.int16, (height, n), 0))


def split3(x):
    a = x.astype(BF).astype(F32)
    r = x - a
    b = r.astype(BF).astype(F32)
    return a, b, r - b


def lift(geometry, right):
    a, b, c = split3(geometry)
    return mm_tn(jnp.concatenate([a, a, b, b, a, c], axis=0).astype(BF), right)


def lift_right(weight):
    a, b, c = split3(weight)
    return jnp.concatenate([a, b, a, b, c, a], axis=0).astype(BF)


def half_silu(half):
    return half + half * jnp.tanh(half)


def norm(v):
    c = v - jnp.mean(v, axis=-1, keepdims=True)
    return c * lax.rsqrt(jnp.mean(c * c, axis=-1, keepdims=True) + 1e-05)


def node_update(latent, total, w_self, w_total, w_out):
    inner = mm(latent, w_self) + mm(total.astype(BF), w_total)
    hidden = half_silu(inner * 0.5).astype(BF)
    return (latent.astype(F32) + norm(mm(hidden, w_out))).astype(BF)


def pick_rows(row, table):
    rows = table.shape[0]
    wide = -(-rows // 128) * 128
    if wide > rows:
        table = jnp.concatenate([table, jnp.zeros((wide - rows, table.shape[1]), BF)], axis=0)
    parts = []
    for at in range(0, row.shape[1], BLOCK):
        cut = row[:, at:at + BLOCK]
        parts.append(mm(pick_matrix(to_columns(cut), wide), table).astype(BF))
    return jnp.concatenate(parts, axis=0) if len(parts) > 1 else parts[0]


def lanes(ref, at, count):
    return jnp.concatenate([ref[r:r + 1, :] for r in range(at // 128, (at + count) // 128)], axis=1)


class Held:
    def __init__(self, sems, **pairs):
        self.copies, self.refs = {}, {}
        for at, (name, (src, dst)) in enumerate(pairs.items()):
            self.refs[name] = dst
            self.copies[name] = pltpu.make_async_copy(src, dst, sems.at[at])
            self.copies[name].start()

    def __call__(self, name):
        if name in self.copies:
            self.copies.pop(name).wait()
        return self.refs[name]


def turned(index, count, me):
    return lax.bitwise_and(index - me, count - 1)


def row_of(rows, at):
    out = None
    for s in range(rows.shape[0]):
        part = jnp.where(at == s, rows[s:s + 1, :], 0)
        out = part if out is None else out + part
    return out


def rows_from(rows, me):
    count = rows.shape[0]
    return jnp.concatenate([row_of(rows, lax.bitwise_and(me - dz, count - 1)) for dz in range(count)], axis=1)


def rows_to(rows, me):
    count = rows.shape[0]
    return jnp.concatenate([row_of(rows, lax.bitwise_and(me + dz, count - 1)) for dz in range(count)], axis=1)


def slot_sums(slot, part, n_mesh, message, outs):
    count = outs[0].shape[0]
    band = n_mesh * count
    me = lax.axis_index("mesh")
    local = slot - part * band
    turn = turned(lax.div(local, count), n_mesh, me) * count + lax.bitwise_and(local, count - 1)
    turn = jnp.where((local >= 0) & (local < band), turn, -1)
    total = mm(add_matrix(turn, band), message)
    for dz in range(n_mesh):
        outs[dz][...] = total[dz * count:(dz + 1) * count].astype(BF)


def encode_kernel(
    count_ref, grid_hbm, src_hbm, slot_hbm, geo_hbm, w_hbm, lift_hbm, feeds_hbm, returns_hbm, message_ref, slot_out, rows_out, *rest
):
    outs, (grid_ref, src_ref, slot_ref, geo_ref, w0_ref, w1_ref, lift_ref, table_ref, sems) = rest[:4], rest[4:]
    held = Held(
        sems, grid=(grid_hbm, grid_ref), w0=(w_hbm.at[0], w0_ref), src=(src_hbm, src_ref), geo=(geo_hbm, geo_ref),
        lift=(lift_hbm, lift_ref), w1=(w_hbm.at[1], w1_ref), slot=(slot_hbm, slot_ref),
        feeds=(feeds_hbm.at[1], rows_out.at[0]), returns=(returns_hbm.at[1], rows_out.at[1]),
    )
    edges = message_ref.shape[0]
    grid = held("grid")[...]
    table_ref[...] = (mm(grid, held("w0")[...]) * 0.5).astype(BF)
    nodes = grid.shape[0]
    held("src"), held("geo"), held("w1")
    right = lift_right(held("lift")[...] * 0.5)
    for at in range(0, edges, BLOCK):
        cut = slice(at, at + BLOCK)
        half = mm(pick_matrix(to_columns(lanes(src_ref, at, BLOCK)), nodes), table_ref[...]) + lift(geo_ref[:, cut], right)
        message_ref[cut, :] = norm(mm(half_silu(half).astype(BF), w1_ref[...])).astype(BF)
    slot = lanes(held("slot"), 0, edges)
    slot = jnp.where(lax.broadcasted_iota(jnp.int32, slot.shape, 1) < count_ref[0], slot, -1)
    slot_out[...] = slot
    held("feeds"), held("returns")
    slot_sums(slot, 1, len(outs), message_ref[...], outs)


def near_kernel(message_ref, slot_ref, *outs):
    slot_sums(slot_ref[...], 0, len(outs), message_ref[...], outs)


def far_kernel(*refs):
    *blocks, rows_ref, _, low_ref, high_ref = refs
    rows = rows_from(rows_ref[0], lax.axis_index("mesh"))
    table = jnp.concatenate([b[...] for b in blocks], axis=0)
    total = mm(add_matrix(rows, 2 * low_ref.shape[0]), table).astype(BF)
    low_ref[...] = total[:low_ref.shape[0]]
    high_ref[...] = total[low_ref.shape[0]:]


def first_kernel(*refs):
    *blocks, low_ref, high_ref, rows_ref, halo_ref, latent_hbm, w_hbm, next_hbm, out_ref, sender_ref, sent_ref = refs[:-6]
    latent_ref, wa_ref, wb_ref, wc_ref, wn_ref, sems = refs[-6:]
    held = Held(
        sems, latent=(latent_hbm, latent_ref), wa=(w_hbm.at[2], wa_ref), wb=(w_hbm.at[3], wb_ref),
        wc=(w_hbm.at[4], wc_ref), wn=(next_hbm.at[0, 0], wn_ref),
    )
    rows = rows_from(rows_ref[0], lax.axis_index("mesh"))
    table = jnp.concatenate([b[...] for b in blocks], axis=0)
    total = mm(add_matrix(rows, out_ref.shape[0]), table)
    total = total + jnp.concatenate([low_ref[...], high_ref[...]], axis=0).astype(F32)
    latent = node_update(held("latent")[...], total, held("wa")[...], held("wb")[...], held("wc")[...])
    out_ref[...] = latent
    sender = (mm(latent, held("wn")[...]) * 0.5).astype(BF)
    sender_ref[...] = sender
    sent_ref[...] = pick_rows(halo_ref[...], sender)


def before_kernel(latent_ref, sender_ref, src_hbm, tgt_hbm, geo_hbm, lift_hbm, w_hbm, base_hbm, own_ref, src_out, tgt_out,
                  geo_ref, lift_ref, wb_ref, wd_ref, base_ref, sems, out_sems, *, layer):
    held = Held(
        sems, wb=(w_hbm.at[layer, 1], wb_ref), src=(src_hbm, src_out), tgt=(tgt_hbm, tgt_out), geo=(geo_hbm, geo_ref),
        lift=(lift_hbm.at[layer], lift_ref), wd=(w_hbm.at[layer, 3], wd_ref),
    )
    latent = latent_ref[...]
    rows = latent.shape[0]
    target = (mm(latent, held("wb")[...]) * 0.5).astype(BF)
    wide = -(-2 * rows // 128) * 128
    pieces = [sender_ref[...], target]
    if wide > 2 * rows:
        pieces.append(jnp.zeros((wide - 2 * rows, latent.shape[1]), BF))
    table = jnp.concatenate(pieces, axis=0)
    held("src"), held("tgt"), held("geo")
    right = lift_right(held("lift")[...] * 0.5)
    sent = []
    for at in range(0, base_ref.shape[0], BLOCK):
        cut = slice(at, at + BLOCK)
        src = lanes(src_out, at, BLOCK)
        src_col = to_columns(jnp.where(src < rows, src, -1)).astype(jnp.int16)
        tgt_col = to_columns(lanes(tgt_out, at, BLOCK) + rows).astype(jnp.int16)
        groups = [as_ones(lane_hits(src_col, lane) | lane_hits(tgt_col, lane)) for lane in range(0, wide, 128)]
        base_ref[cut, :] = mm(jnp.concatenate(groups, axis=1), table) + lift(geo_ref[:, cut], right)
        sent.append(pltpu.make_async_copy(base_ref.at[cut, :], base_hbm.at[cut, :], out_sems.at[at // BLOCK]))
        sent[-1].start()
    own_ref[...] = mm(latent, held("wd")[...])
    for copy in sent:
        copy.wait()


def layer_kernel(latent_ref, came_ref, base_hbm, own_ref, src_ref, tgt_ref, pick_ref, w_hbm, next_hbm, *rest, layer, last):
    outs, (message_ref, wc_ref, we_ref, wf_ref, wn_ref, base_ref, sems, in_sems) = rest[:-8], rest[-8:]
    cuts = [slice(at, at + BLOCK) for at in range(0, base_ref.shape[0], BLOCK)]
    bases = Held(in_sems, **{f"b{i}": (base_hbm.at[cut, :], base_ref.at[cut, :]) for i, cut in enumerate(cuts)})
    held = Held(
        sems, wc=(w_hbm.at[layer, 2], wc_ref), we=(w_hbm.at[layer, 4], we_ref), wf=(w_hbm.at[layer, 5], wf_ref),
        wn=(next_hbm.at[0] if last else next_hbm.at[layer + 1, 0], wn_ref),
    )
    latent = latent_ref[...]
    rows = latent.shape[0]
    halo = came_ref.shape[0]
    for at in range(0, base_ref.shape[0], BLOCK):
        cut = slice(at, at + BLOCK)
        half = mm(pick_matrix(to_columns(lanes(src_ref, at, BLOCK) - rows), halo), came_ref[...]) + bases(f"b{at // BLOCK}")[...]
        message_ref[cut, :] = norm(mm(half_silu(half).astype(BF), held("wc")[...])).astype(BF)
    total = mm(add_matrix(lanes(tgt_ref, 0, base_ref.shape[0]), rows), message_ref[...])
    inner = own_ref[...] + mm(total.astype(BF), held("we")[...])
    hidden = half_silu(inner * 0.5).astype(BF)
    latent = (latent.astype(F32) + norm(mm(hidden, held("wf")[...]))).astype(BF)
    outs[0][...] = latent
    onward = mm(latent, held("wn")[...])
    if last:
        onward = onward.astype(BF)
        outs[1][...] = onward
        spread(rows_to(pick_ref[0], lax.axis_index("mesh")), onward, outs[2:])
    else:
        onward = (onward * 0.5).astype(BF)
        outs[1][...] = onward
        outs[2][...] = pick_rows(pick_ref[...], onward)


def spread(row, table, outs):
    picked = pick_rows(row, table)
    count = outs[0].shape[0]
    for dz, out in enumerate(outs):
        out[...] = picked[dz * count:(dz + 1) * count]


def spread_kernel(table_ref, rows_ref, *outs):
    spread(rows_to(rows_ref[1], lax.axis_index("mesh")), table_ref[...], outs)


def place_columns(place, part, n_mesh, count):
    me = lax.axis_index("mesh")
    local = place - part * n_mesh * count
    turn = lax.bitwise_and(me - lax.div(local, count), n_mesh - 1) * count + lax.bitwise_and(local, count - 1)
    return to_columns(jnp.where((local >= 0) & (local < n_mesh * count), turn, -1))


def decode_near_kernel(*refs):
    *blocks, grid_hbm, src_hbm, geo_hbm, lift_hbm, w_hbm, base_ref, grid_ref, src_ref, geo_ref, lift_ref, w_ref, own_ref, sems = refs
    held = Held(
        sems, grid=(grid_hbm, grid_ref), w=(w_hbm.at[1], w_ref), src=(src_hbm, src_ref), geo=(geo_hbm, geo_ref),
        lift=(lift_hbm, lift_ref),
    )
    own_ref[...] = mm(held("grid")[...], held("w")[...]) * 0.5
    table = jnp.concatenate([b[...] for b in blocks], axis=0) * 0.5
    count = blocks[0].shape[0]
    right = lift_right(held("lift")[...] * 0.5)
    held("src"), held("geo")
    for at in range(0, own_ref.shape[0], BLOCK):
        cut = slice(at, at + BLOCK)
        for which in range(src_ref.shape[0]):
            columns = place_columns(src_ref[which:which + 1, cut], 0, len(blocks), count)
            chosen = mm(pick_matrix(columns, table.shape[0]), table)
            base_ref[which, cut, :] = chosen + lift(geo_ref[which, :, cut], right) + own_ref[cut, :]


def decode_kernel(*refs):
    *blocks, base_ref, grid_hbm, src_hbm, w_hbm, out_ref, grid_ref, src_ref, w_ref, sems = refs
    held = Held(sems, src=(src_hbm, src_ref), w=(w_hbm.at[2], w_ref), grid=(grid_hbm, grid_ref))
    table = jnp.concatenate([b[...] for b in blocks], axis=0) * 0.5
    count = blocks[0].shape[0]
    held("src")
    for at in range(0, out_ref.shape[0], BLOCK):
        cut = slice(at, at + BLOCK)
        hidden = None
        for which in range(src_ref.shape[0]):
            columns = place_columns(src_ref[which:which + 1, cut], 1, len(blocks), count)
            more = half_silu(base_ref[which, cut, :] + mm(pick_matrix(columns, table.shape[0]), table))
            hidden = more if hidden is None else hidden + more
        update = norm(mm(hidden.astype(BF), held("w")[...]))
        out_ref[cut, :] = (held("grid")[cut, :].astype(F32) + update).astype(BF)


def call(kernel, name, out, specs, args, scratch=(), flops=0, limit=24, outs=None, copies=0):
    if scratch:
        scratch = list(scratch) + [pltpu.SemaphoreType.DMA((16,))]
    if copies:
        scratch.append(pltpu.SemaphoreType.DMA((copies,)))
    args = [pltpu.with_memory_space_constraint(a, pltpu.HBM) if s is HB else a for s, a in zip(specs, args)]
    return pl.pallas_call(
        kernel,
        out_shape=out,
        in_specs=specs,
        out_specs=jax.tree.map(lambda _: VM, out) if outs is None else tuple(outs),
        scratch_shapes=scratch,
        compiler_params=pltpu.CompilerParams(vmem_limit_bytes=limit * MIB),
        cost_estimate=pl.CostEstimate(flops=flops, bytes_accessed=4 * MIB, transcendentals=0),
        name=name,
    )(*args)


def strip_shift(value, by):
    length = lax.axis_size("grid")
    pairs = [(i, i + by) for i in range(length) if 0 <= i + by < length]
    return lax.ppermute(value, "grid", pairs)


def exchange(blocks):
    length = len(blocks)
    moved = [blocks[0]]
    for dz in range(1, length):
        moved.append(lax.ppermute(blocks[dz], "mesh", [(i, (i + dz) % length) for i in range(length)]))
    return moved


def shards(
    grid_latent,
    mesh_latent,
    enc_source,
    enc_slot,
    enc_geometry,
    edge_count,
    slot_row,
    halo_rows,
    proc_source,
    proc_target,
    proc_geometry,
    return_rows,
    dec_source,
    dec_geometry,
    enc_weights,
    enc_lift,
    proc_weights,
    proc_lift,
    dec_weights,
    dec_lift,
):
    nodes, width = grid_latent.shape
    mesh_rows = mesh_latent.shape[0]
    n_mesh = lax.axis_size("mesh")
    count = slot_row.shape[3]
    edges, links = enc_source.shape[0], proc_source.shape[0]
    near_of = dec_source.shape[1]
    shape = jax.ShapeDtypeStruct
    block = shape((count, width), BF)
    row = shape((mesh_rows, width), BF)
    square = pltpu.VMEM((width, width), BF)
    lifts = pltpu.VMEM(enc_lift.shape, F32)
    message, slot, above, *far = call(
        encode_kernel, "encode", (shape((edges, width), BF), shape((1, edges), jnp.int32), shape((2, n_mesh, count), jnp.int32)) + (block,) * n_mesh,
        [SM] + [HB] * 8,
        (edge_count, grid_latent, enc_source.reshape(-1, 128), enc_slot.reshape(-1, 128), enc_geometry, enc_weights, enc_lift, slot_row[0], return_rows[0]),
        [pltpu.VMEM((nodes, width), BF), pltpu.VMEM((edges // 128, 128), jnp.int32), pltpu.VMEM((edges // 128, 128), jnp.int32),
         pltpu.VMEM((4, edges), F32), square, square, lifts, pltpu.VMEM((nodes, width), BF)],
        flops=5 * 10**9,
    )
    above = strip_shift(above, -1)
    far = exchange(far)
    near = call(near_kernel, "near", (block,) * n_mesh, [VM] * 2, (message, slot), flops=10**9)
    half = shape((mesh_rows // 2, width), BF)
    up = call(far_kernel, "far", (half, half), [VM] * (n_mesh + 1) + [ANY], (*far, above, near[0]), flops=10**8)
    near = exchange(near)
    cut = mesh_rows // 2
    up = [strip_shift(up[0], 1), strip_shift(up[1], 1)]
    halo = halo_rows.reshape(1, -1)
    sends = shape((halo.shape[1], width), BF)
    latent, sender, sent = call(
        first_kernel, "first", (row, row, sends), [VM] * (n_mesh + 4) + [HB] * 3,
        (*near, *up, slot_row[0], halo, mesh_latent, enc_weights, proc_weights),
        [pltpu.VMEM((mesh_rows, width), BF)] + [square] * 4, flops=10**9,
    )
    layers = proc_weights.shape[0]
    index = shape((links // 128, 128), jnp.int32)
    for layer in range(layers):
        came = lax.all_to_all(
            sent.reshape(lax.axis_size("grid") * n_mesh, -1, width), ("grid", "mesh"), split_axis=0, concat_axis=0, tiled=True
        ).reshape(sent.shape)
        base, own, src, tgt = call(
            functools.partial(before_kernel, layer=layer), "before",
            (pltpu.HBM((links, width), F32), shape((mesh_rows, width), F32), index, index), [VM] * 2 + [HB] * 5,
            (latent, sender, proc_source.reshape(-1, 128), proc_target.reshape(-1, 128), proc_geometry, proc_lift, proc_weights),
            [pltpu.VMEM((4, links), F32), lifts, square, square, pltpu.VMEM((links, width), F32)],
            flops=10**9, outs=[HB, VM, VM, VM], copies=links // BLOCK,
        )
        last = layer + 1 == layers
        out = call(
            functools.partial(layer_kernel, layer=layer, last=last), "layer",
            (row, row) + ((block,) * n_mesh if last else (sends,)), [VM, VM, HB, VM, VM, VM, VM, HB, HB],
            (latent, came, base, own, src, tgt, return_rows[0] if last else halo, proc_weights,
             dec_weights if last else proc_weights),
            [pltpu.VMEM((links, width), BF)] + [square] * 4 + [pltpu.VMEM((links, width), F32)], flops=4 * 10**9,
            copies=links // BLOCK,
        )
        if last:
            latent, proj, *back = out
        else:
            latent, sender, sent = out
    proj = strip_shift(proj, -1)
    back = exchange(back)
    ahead = exchange(call(spread_kernel, "spread", (block,) * n_mesh, [VM] * 2, (proj, above), flops=10**8))
    sources = dec_source.T
    base = call(
        decode_near_kernel, "decode_near", shape((near_of, nodes, width), F32), [VM] * n_mesh + [HB] * 5,
        (*back, grid_latent, sources, dec_geometry.transpose(1, 0, 2), dec_lift, dec_weights),
        [pltpu.VMEM((nodes, width), BF), pltpu.VMEM((near_of, nodes), jnp.int32), pltpu.VMEM((near_of, 4, nodes), F32),
         lifts, square, pltpu.VMEM((nodes, width), F32)],
        flops=3 * 10**9,
    )
    grid_out = call(
        decode_kernel, "decode", shape(grid_latent.shape, BF), [VM] * (n_mesh + 1) + [HB] * 3,
        (*ahead, base, grid_latent, sources, dec_weights),
        [pltpu.VMEM((nodes, width), BF), pltpu.VMEM((near_of, nodes), jnp.int32), square],
        flops=3 * 10**9,
    )
    return (grid_out, latent)


def solution(mesh):
    placed = (
        P(("grid", "mesh"), None),
        P(("grid", "mesh"), None),
        P(("grid", "mesh")),
        P(("grid", "mesh")),
        P(None, ("grid", "mesh")),
        P(("grid", "mesh")),
        P(("grid", "mesh"), None, None, None),
        P(("grid", "mesh"), None, None),
        P(("grid", "mesh")),
        P(("grid", "mesh")),
        P(None, ("grid", "mesh")),
        P(("grid", "mesh"), None, None, None),
        P(("grid", "mesh"), None),
        P(None, None, ("grid", "mesh")),
        P(),
        P(),
        P(),
        P(),
        P(),
        P(),
    )
    return jax.shard_map(
        shards,
        mesh=mesh,
        in_specs=placed,
        out_specs=(P(("grid", "mesh"), None), P(("grid", "mesh"), None)),
        check_vma=False,
    )
```

```python
import functools

import jax
import jax.numpy as jnp
from jax import lax
from jax.experimental import pallas as pl
from jax.experimental.pallas import tpu as pltpu
from jax.sharding import PartitionSpec as P

BF = jnp.bfloat16
F32 = jnp.float32
VM = pl.BlockSpec(memory_space=pltpu.VMEM)
SM = pl.BlockSpec(memory_space=pltpu.SMEM)
HB = pl.BlockSpec(memory_space=pltpu.HBM)
ANY = pl.BlockSpec(memory_space=pl.ANY)
MIB = 1024 * 1024
BLOCK = 512


def mm(a, b):
    return lax.dot_general(a, b, (((1,), (0,)), ((), ())), preferred_element_type=F32)


def mm_tn(a, b):
    return lax.dot_general(a, b, (((0,), (0,)), ((), ())), preferred_element_type=F32)


def to_columns(row):
    n = row.shape[1]
    parts = [jnp.broadcast_to(row[:, at:at + 128], (128, 128)).T for at in range(0, n, 128)]
    return jnp.concatenate(parts, axis=0) if len(parts) > 1 else parts[0]


def lane_hits(columns, at):
    return columns - jnp.int16(at) == lax.broadcasted_iota(jnp.int16, columns.shape, 1)


def as_ones(hits):
    return jnp.where(hits, jnp.ones(hits.shape, BF), jnp.zeros(hits.shape, BF))


def pick_matrix(columns, width):
    col = columns.astype(jnp.int16)
    return jnp.concatenate([as_ones(lane_hits(col, at)) for at in range(0, width, 128)], axis=1)


def add_matrix(row, height):
    n = row.shape[1]
    wide = jnp.broadcast_to(row, (16, n)).astype(jnp.int16)
    wide = jnp.broadcast_to(wide[None], (height // 16, 16, n)).reshape(height, n)
    return as_ones(wide == lax.broadcasted_iota(jnp.int16, (height, n), 0))


def split3(x):
    a = x.astype(BF).astype(F32)
    r = x - a
    b = r.astype(BF).astype(F32)
    return a, b, r - b


def lift(geometry, right):
    a, b, c = split3(geometry)
    return mm_tn(jnp.concatenate([a, a, b, b, a, c], axis=0).astype(BF), right)


def lift_right(weight):
    a, b, c = split3(weight)
    return jnp.concatenate([a, b, a, b, c, a], axis=0).astype(BF)


def half_silu(half):
    return half + half * jnp.tanh(half)


def centered(weight):
    wide = weight.astype(F32)
    return (wide - jnp.mean(wide, axis=-1, keepdims=True)).astype(BF)


def scaled(v):
    return v * lax.rsqrt(jnp.mean(v * v, axis=-1, keepdims=True) + 1e-05)


def norm(v):
    c = v - jnp.mean(v, axis=-1, keepdims=True)
    return c * lax.rsqrt(jnp.mean(c * c, axis=-1, keepdims=True) + 1e-05)


def node_update(latent, own, total, w_total, w_out):
    inner = own + mm(total.astype(BF), w_total)
    hidden = half_silu(inner * 0.5).astype(BF)
    return (latent.astype(F32) + scaled(mm(hidden, w_out))).astype(BF)


def padded(table, rows):
    return jnp.concatenate([table, jnp.zeros((rows - table.shape[0], table.shape[1]), BF)], axis=0)


def pick_rows(row, table):
    wide = -(-table.shape[0] // 128) * 128
    return mm(pick_matrix(to_columns(row), wide), padded(table, wide)).astype(BF)


def lanes(ref, at, count):
    return jnp.concatenate([ref[r:r + 1, :] for r in range(at // 128, (at + count) // 128)], axis=1)


class Held:
    def __init__(self, sems, **pairs):
        self.copies, self.refs = {}, {}
        for at, (name, (src, dst)) in enumerate(pairs.items()):
            self.refs[name] = dst
            self.copies[name] = pltpu.make_async_copy(src, dst, sems.at[at])
            self.copies[name].start()

    def __call__(self, name):
        if name in self.copies:
            self.copies.pop(name).wait()
        return self.refs[name]


class Sent:
    def __init__(self, sems):
        self.sems, self.copies = sems, []

    def __call__(self, src, dst):
        self.copies.append(pltpu.make_async_copy(src, dst, self.sems.at[len(self.copies)]))
        self.copies[-1].start()

    def wait(self):
        for copy in self.copies:
            copy.wait()


def turned(index, count, me):
    return lax.bitwise_and(index - me, count - 1)


def row_of(rows, at):
    out = None
    for s in range(rows.shape[0]):
        part = jnp.where(at == s, rows[s:s + 1, :], 0)
        out = part if out is None else out + part
    return out


def rows_from(rows, me):
    count = rows.shape[0]
    return jnp.concatenate([row_of(rows, lax.bitwise_and(me - dz, count - 1)) for dz in range(count)], axis=1)


def rows_to(rows, me):
    count = rows.shape[0]
    return jnp.concatenate([row_of(rows, lax.bitwise_and(me + dz, count - 1)) for dz in range(count)], axis=1)


def slot_sums(slot, part, n_mesh, message, outs):
    count = outs[0].shape[0]
    band = n_mesh * count
    me = lax.axis_index("mesh")
    local = slot - part * band
    turn = turned(lax.div(local, count), n_mesh, me) * count + lax.bitwise_and(local, count - 1)
    turn = jnp.where((local >= 0) & (local < band), turn, -1)
    total = mm(add_matrix(turn, band), message)
    for dz in range(n_mesh):
        outs[dz][...] = total[dz * count:(dz + 1) * count].astype(BF)


def encode_kernel(count_ref, grid_hbm, src_hbm, slot_hbm, geo_hbm, w_hbm, lift_hbm, message_ref, slot_out, *rest):
    outs, (grid_ref, src_ref, slot_ref, geo_ref, w0_ref, w1_ref, lift_ref, table_ref, sems) = rest[:4], rest[4:]
    nodes, edges = grid_ref.shape[0], message_ref.shape[0]
    cuts = [slice(at, at + 256) for at in range(0, nodes, 256)]
    held = Held(
        sems, w0=(w_hbm.at[0], w0_ref), **{f"g{i}": (grid_hbm.at[cut, :], grid_ref.at[cut, :]) for i, cut in enumerate(cuts)},
        src=(src_hbm, src_ref), geo=(geo_hbm, geo_ref), lift=(lift_hbm, lift_ref), w1=(w_hbm.at[1], w1_ref),
        slot=(slot_hbm, slot_ref),
    )
    held("w0")
    for i, cut in enumerate(cuts):
        table_ref[cut, :] = (mm(held(f"g{i}")[...], w0_ref[...]) * 0.5).astype(BF)
    held("src"), held("geo"), held("w1")
    right = lift_right(held("lift")[...] * 0.5)
    for at in range(0, edges, BLOCK):
        cut = slice(at, at + BLOCK)
        half = mm(pick_matrix(to_columns(lanes(src_ref, at, BLOCK)), nodes), table_ref[...]) + lift(geo_ref[:, cut], right)
        message_ref[cut, :] = norm(mm(half_silu(half).astype(BF), w1_ref[...])).astype(BF)
    slot = lanes(held("slot"), 0, edges)
    slot = jnp.where(lax.broadcasted_iota(jnp.int32, slot.shape, 1) < count_ref[0], slot, -1)
    slot_out[...] = slot
    slot_sums(slot, 1, len(outs), message_ref[...], outs)


def near_kernel(message_ref, slot_ref, halo_hbm, latent_hbm, w_hbm, next_hbm, *rest):
    outs, (latent_out, own_ref, wb_out, wc_out, wn_out, hot_ref, hot_hbm, halo_ref, wa_ref, wc_ref, sems, out_sems) = rest[:4], rest[4:]
    held = Held(
        sems, halo=(halo_hbm, halo_ref), latent=(latent_hbm, latent_out), wa=(w_hbm.at[2], wa_ref), wc=(w_hbm.at[4], wc_ref),
        wb=(w_hbm.at[3], wb_out), wn=(next_hbm.at[0, 0], wn_out),
    )
    slot_sums(slot_ref[...], 0, len(outs), message_ref[...], outs)
    halo = held("halo")[...].astype(F32).astype(BF)
    places, owners = halo.shape
    row = lax.broadcasted_iota(jnp.int32, (places * owners, 128), 0)
    lane = lax.broadcasted_iota(jnp.int32, row.shape, 1)
    owner = jnp.where(lax.div(row, places) == lane, 1.0, 0.0).astype(BF)
    each = lax.dot_general(owner, halo, (((1,), (1,)), ((), ())), preferred_element_type=F32)
    mine = jnp.where(lax.bitwise_and(row, places - 1)[:, :places] == lane[:, :places], each, 0.0)
    column = jnp.broadcast_to(jnp.sum(mine, axis=1, keepdims=True), row.shape).astype(jnp.int32)
    hot_ref[...] = pick_matrix(column, hot_ref.shape[1])
    sent = Sent(out_sems)
    sent(hot_ref, hot_hbm)
    own_ref[...] = mm(held("latent")[...], held("wa")[...])
    wc_out[...] = centered(held("wc")[...])
    held("wb"), held("wn")
    sent.wait()


def far_kernel(*refs):
    *blocks, rows_ref, _, low_ref, high_ref = refs
    rows = rows_from(rows_ref[1], lax.axis_index("mesh"))
    table = jnp.concatenate([b[...] for b in blocks], axis=0)
    total = mm(add_matrix(rows, 2 * low_ref.shape[0]), table).astype(BF)
    low_ref[...] = total[:low_ref.shape[0]]
    high_ref[...] = total[low_ref.shape[0]:]


def first_kernel(*refs):
    *blocks, low_ref, high_ref, rows_ref, latent_ref, own_ref, wb_ref, wc_ref, wn_ref, hot_ref, out_ref, sender_ref, sent_ref = refs
    rows = rows_from(rows_ref[0], lax.axis_index("mesh"))
    table = jnp.concatenate([b[...] for b in blocks], axis=0)
    total = mm(add_matrix(rows, out_ref.shape[0]), table)
    total = total + jnp.concatenate([low_ref[...], high_ref[...]], axis=0).astype(F32)
    latent = node_update(latent_ref[...], own_ref[...], total, wb_ref[...], wc_ref[...])
    out_ref[...] = latent
    sender = (mm(latent, wn_ref[...]) * 0.5).astype(BF)
    sender_ref[...] = sender
    sent_ref[...] = mm(hot_ref[...], padded(sender, hot_ref.shape[1])).astype(BF)


def before_kernel(latent_ref, sender_ref, src_hbm, tgt_hbm, geo_hbm, lift_hbm, w_hbm, *rest, layer, last):
    if last:
        (grid_hbm, decgeo_hbm, declift_hbm, dec_hbm), rest = rest[:4], rest[4:]
        (*shares, decw_out), rest = rest[:4], rest[4:]
    own_ref, src_ref, tgt_ref, *bases = rest[:5]
    (wc_out, wf_out), rest = rest[5:7], rest[7:]
    if last:
        (grid_ref, decgeo_ref, declift_ref, decv_ref, decw_ref, total_ref, share_ref), rest = rest[:7], rest[7:]
    geo_ref, lift_ref, wb_ref, wd_ref, wc_ref, wf_ref, sems, out_sems = rest
    more = {}
    if last:
        more = dict(
            grid=(grid_hbm, grid_ref), decgeo=(decgeo_hbm, decgeo_ref), declift=(declift_hbm, declift_ref),
            decv=(dec_hbm.at[1], decv_ref), decw=(dec_hbm.at[2], decw_ref),
        )
    held = Held(
        sems, wb=(w_hbm.at[layer, 1], wb_ref), src=(src_hbm, src_ref), tgt=(tgt_hbm, tgt_ref), geo=(geo_hbm, geo_ref),
        lift=(lift_hbm.at[layer], lift_ref), wd=(w_hbm.at[layer, 3], wd_ref), wc=(w_hbm.at[layer, 2], wc_ref),
        wf=(w_hbm.at[layer, 5], wf_ref), **more,
    )
    sent = Sent(out_sems)
    latent = latent_ref[...]
    rows = latent.shape[0]
    target = (mm(latent, held("wb")[...]) * 0.5).astype(BF)
    wide = -(-2 * rows // 128) * 128
    table = padded(jnp.concatenate([sender_ref[...], target], axis=0), wide)
    held("src"), held("tgt"), held("geo")
    right = lift_right(held("lift")[...] * 0.5)
    for part, base_ref in enumerate(bases):
        for at in range(0, base_ref.shape[0], 128):
            near = part * base_ref.shape[0] + at
            src = to_columns(lanes(src_ref, near, 128))
            src_col = jnp.where(src < rows, src, -1).astype(jnp.int16)
            tgt_col = to_columns(lanes(tgt_ref, near, 128) + rows).astype(jnp.int16)
            groups = [as_ones(lane_hits(src_col, lane) | lane_hits(tgt_col, lane)) for lane in range(0, wide, 128)]
            base = mm(jnp.concatenate(groups, axis=1), table) + lift(geo_ref[:, near:near + 128], right)
            base_ref[at:at + 128, :] = base.astype(BF)
    own_ref[...] = mm(latent, held("wd")[...])
    wc_ref[...] = centered(held("wc")[...])
    sent(wc_ref, wc_out)
    wf_ref[...] = centered(held("wf")[...])
    sent(wf_ref, wf_out)
    if last:
        right = lift_right(held("declift")[...] * 0.5)
        total_ref[...] = mm(held("grid")[...], held("decv")[...]) * 0.5
        decw_ref[...] = centered(held("decw")[...])
        sent(decw_ref, decw_out)
        held("decgeo")
        for which, out in enumerate(shares):
            for at in range(0, out.shape[0], 256):
                cut = slice(at, at + 256)
                share_ref[which, cut, :] = (lift(decgeo_ref[which, :, cut], right) + total_ref[cut, :]).astype(BF)
            sent(share_ref.at[which], out)
    sent.wait()


def layer_kernel(latent_ref, came_ref, own_ref, src_ref, tgt_ref, *rest, layer, last):
    (*bases, wc_hbm, wf_hbm, w_hbm, next_hbm, pick_ref, _), rest = rest[:8], rest[8:]
    outs, (message_ref, wc_ref, we_ref, wf_ref, wn_ref, hot_ref, sems) = rest[:-7], rest[-7:]
    more = {} if last else dict(hot=(pick_ref, hot_ref))
    held = Held(
        sems, wc=(wc_hbm, wc_ref), we=(w_hbm.at[layer, 4], we_ref), wf=(wf_hbm, wf_ref),
        wn=(next_hbm.at[0] if last else next_hbm.at[layer + 1, 0], wn_ref), **more,
    )
    rows = latent_ref.shape[0]
    for part, base_ref in enumerate(bases):
        count = base_ref.shape[0]
        hits = pick_matrix(to_columns(lanes(src_ref, part * count, count) - rows), came_ref.shape[0])
        half = mm(hits, came_ref[...]) + base_ref[...].astype(F32)
        message = scaled(mm(half_silu(half).astype(BF), held("wc")[...]))
        message_ref[part * count:(part + 1) * count, :] = message.astype(BF)
    total = mm(add_matrix(lanes(tgt_ref, 0, message_ref.shape[0]), rows), message_ref[...])
    latent = node_update(latent_ref[...], own_ref[...], total, held("we")[...], held("wf")[...])
    outs[0][...] = latent
    onward = mm(latent, held("wn")[...])
    if last:
        onward = onward.astype(BF)
        outs[1][...] = onward
        spread(rows_to(pick_ref[0], lax.axis_index("mesh")), onward, outs[2:])
    else:
        onward = (onward * 0.5).astype(BF)
        outs[1][...] = onward
        outs[2][...] = mm(held("hot")[...], padded(onward, hot_ref.shape[1])).astype(BF)


def spread(row, table, outs):
    picked = pick_rows(row, table)
    count = outs[0].shape[0]
    for dz, out in enumerate(outs):
        out[...] = picked[dz * count:(dz + 1) * count]


def spread_kernel(table_ref, rows_ref, *outs):
    spread(rows_to(rows_ref[1], lax.axis_index("mesh")), table_ref[...], outs)


def place_columns(place, part, n_mesh, count):
    me = lax.axis_index("mesh")
    local = place - part * n_mesh * count
    turn = lax.bitwise_and(me - lax.div(local, count), n_mesh - 1) * count + lax.bitwise_and(local, count - 1)
    return to_columns(jnp.where((local >= 0) & (local < n_mesh * count), turn, -1))


def decode_near_kernel(*refs):
    *blocks, dec0, dec1, dec2, src_hbm, base_ref, hot0, hot1, hot2, src_ref, share_ref, sems = refs
    held = Held(sems, src=(src_hbm, src_ref), **{
        f"d{i}": (dec, share_ref.at[i]) for i, dec in enumerate((dec0, dec1, dec2))
    })
    table = jnp.concatenate([b[...] for b in blocks], axis=0) * 0.5
    count = blocks[0].shape[0]
    held("src")
    for which, hot in enumerate((hot0, hot1, hot2)):
        for at in range(0, base_ref.shape[1], BLOCK):
            cut = slice(at, at + BLOCK)
            place = src_ref[which:which + 1, cut]
            hits = pick_matrix(place_columns(place, 0, len(blocks), count), table.shape[0])
            near = mm(hits, table)
            held(f"d{which}")
            base_ref[which, cut, :] = near + share_ref[which, cut, :].astype(F32)
            hot[cut, :] = pick_matrix(place_columns(place, 1, len(blocks), count), table.shape[0])


def decode_kernel(*refs):
    *blocks, base_ref, hot0, hot1, hot2, w_hbm, grid_hbm, out_hbm, w_ref, grid_ref, out_ref, sems, out_sems = refs
    held = Held(sems, w=(w_hbm, w_ref), grid=(grid_hbm, grid_ref))
    table = jnp.concatenate([b[...] for b in blocks], axis=0) * 0.5
    step = out_ref.shape[0] // out_sems.shape[0]
    sent = []
    for at in range(0, out_ref.shape[0], step):
        cut = slice(at, at + step)
        hidden = None
        for which, hot in enumerate((hot0, hot1, hot2)):
            more = half_silu(base_ref[which, cut, :] + mm(hot[cut, :], table))
            hidden = more if hidden is None else hidden + more
        update = scaled(mm(hidden.astype(BF), held("w")[...]))
        out_ref[cut, :] = (held("grid")[cut, :].astype(F32) + update).astype(BF)
        sent.append(pltpu.make_async_copy(out_ref.at[cut, :], out_hbm.at[cut, :], out_sems.at[at // step]))
        sent[-1].start()
    for copy in sent:
        copy.wait()


def call(kernel, name, out, specs, args, scratch=(), flops=0, limit=24, outs=None, copies=0, wait=True):
    if scratch and wait:
        scratch = list(scratch) + [pltpu.SemaphoreType.DMA((16,))]
    if copies:
        scratch.append(pltpu.SemaphoreType.DMA((copies,)))
    args = [pltpu.with_memory_space_constraint(a, pltpu.HBM) if s is HB else a for s, a in zip(specs, args)]
    return pl.pallas_call(
        kernel,
        out_shape=out,
        in_specs=specs,
        out_specs=jax.tree.map(lambda _: VM, out) if outs is None else outs,
        scratch_shapes=scratch,
        compiler_params=pltpu.CompilerParams(vmem_limit_bytes=limit * MIB),
        cost_estimate=pl.CostEstimate(flops=flops, bytes_accessed=4 * MIB, transcendentals=0),
        name=name,
    )(*args)


def strip_shift(value, by):
    length = lax.axis_size("grid")
    pairs = [(i, i + by) for i in range(length) if 0 <= i + by < length]
    return lax.ppermute(value, "grid", pairs)


def exchange(blocks):
    length = len(blocks)
    moved = [blocks[0]]
    for dz in range(1, length):
        moved.append(lax.ppermute(blocks[dz], "mesh", [(i, (i + dz) % length) for i in range(length)]))
    return moved


def shards(
    grid_latent,
    mesh_latent,
    enc_source,
    enc_slot,
    enc_geometry,
    edge_count,
    slot_row,
    halo_rows,
    proc_source,
    proc_target,
    proc_geometry,
    return_rows,
    dec_source,
    dec_geometry,
    enc_weights,
    enc_lift,
    proc_weights,
    proc_lift,
    dec_weights,
    dec_lift,
):
    nodes, width = grid_latent.shape
    mesh_rows = mesh_latent.shape[0]
    n_mesh = lax.axis_size("mesh")
    count = slot_row.shape[3]
    edges, links = enc_source.shape[0], proc_source.shape[0]
    near_of = dec_source.shape[1]
    shape = jax.ShapeDtypeStruct
    block = shape((count, width), BF)
    row = shape((mesh_rows, width), BF)
    wide_row = shape((mesh_rows, width), F32)
    weight = shape((width, width), BF)
    square = pltpu.VMEM((width, width), BF)
    lifts = pltpu.VMEM(enc_lift.shape, F32)
    above = strip_shift(slot_row[0], -1)
    message, slot, *far = call(
        encode_kernel, "encode", (shape((edges, width), BF), shape((1, edges), jnp.int32)) + (block,) * n_mesh, [SM] + [HB] * 6,
        (edge_count, grid_latent, enc_source.reshape(-1, 128), enc_slot.reshape(-1, 128), enc_geometry, enc_weights, enc_lift),
        [pltpu.VMEM((nodes, width), BF), pltpu.VMEM((edges // 128, 128), jnp.int32),
         pltpu.VMEM((edges // 128, 128), jnp.int32), pltpu.VMEM((4, edges), F32), square, square, lifts,
         pltpu.VMEM((nodes, width), BF)],
        flops=5 * 10**9,
    )
    far = exchange(far)
    halo = halo_rows[0].T
    sends = shape((halo.size, width), BF)
    hot = shape((halo.size, -(-mesh_rows // 128) * 128), BF)
    *near, start, own, wb, wc, wn, hot, hot_far = call(
        near_kernel, "near", (block,) * n_mesh + (row, wide_row, weight, weight, weight, hot, pltpu.HBM(hot.shape, BF)),
        [VM] * 2 + [HB] * 4, (message, slot, halo, mesh_latent, enc_weights, proc_weights),
        [pltpu.VMEM(halo.shape, jnp.int32), square, square], flops=10**9, outs=(VM,) * (n_mesh + 6) + (HB,), copies=1,
    )
    part = shape((mesh_rows // 2, width), BF)
    up = call(far_kernel, "far", (part, part), [VM] * (n_mesh + 1) + [ANY], (*far, above, near[0]), flops=10**8)
    near = exchange(near)
    up = [strip_shift(up[0], 1), strip_shift(up[1], 1)]
    latent, sender, sent = call(
        first_kernel, "first", (row, row, sends), [VM] * (n_mesh + 9),
        (*near, *up, slot_row[0], start, own, wb, wc, wn, hot), flops=10**9,
    )
    layers = proc_weights.shape[0]
    half = shape((links // 2, width), BF)
    index = shape((links // 128, 128), jnp.int32)
    for layer in range(layers):
        came = lax.all_to_all(
            sent.reshape(lax.axis_size("grid") * n_mesh, -1, width), ("grid", "mesh"), split_axis=0, concat_axis=0, tiled=True
        ).reshape(sent.shape)
        last = layer + 1 == layers
        operands = [
            latent, sender, proc_source.reshape(-1, 128), proc_target.reshape(-1, 128), proc_geometry, proc_lift, proc_weights,
        ]
        outs = (wide_row, index, index, half, half) + (pltpu.HBM(weight.shape, BF),) * 2
        out_specs = (VM,) * 5 + (HB,) * 2
        scratch = [pltpu.VMEM((4, links), F32), lifts, square, square, square, square]
        specs = [VM] * 2 + [HB] * 5
        if last:
            operands += [grid_latent, dec_geometry.transpose(1, 0, 2), dec_lift, dec_weights]
            specs += [HB] * 4
            outs = (pltpu.HBM((nodes, width), BF),) * near_of + (pltpu.HBM(weight.shape, BF),) + outs
            out_specs = (HB,) * (near_of + 1) + out_specs
            scratch = [
                pltpu.VMEM((nodes, width), BF), pltpu.VMEM((near_of, 4, nodes), F32), lifts, square, square,
                pltpu.VMEM((nodes, width), F32), pltpu.VMEM((near_of, nodes, width), BF),
            ] + scratch
        held = list(call(
            functools.partial(before_kernel, layer=layer, last=last), "before", outs, specs, operands, scratch, flops=10**9,
            outs=out_specs, copies=3 + near_of,
        ))
        if last:
            *shares, dec_out = held[:near_of + 1]
            held = held[near_of + 1:]
        if layer == 0:
            places, held[0] = lax.optimization_barrier((return_rows[0], held[0]))
            places = strip_shift(places, -1)
        out = call(
            functools.partial(layer_kernel, layer=layer, last=last), "layer",
            (row, row) + ((block,) * n_mesh if last else (sends,)), [VM] * 7 + [HB] * 4 + [VM if last else HB, ANY],
            (latent, came, *held, proc_weights, dec_weights if last else proc_weights, return_rows[0] if last else hot_far, places),
            [pltpu.VMEM((links, width), BF)] + [square] * 4 + [pltpu.VMEM(hot.shape, BF)], flops=4 * 10**9,
        )
        if last:
            latent, proj, *back = out
        else:
            latent, sender, sent = out
    proj = strip_shift(proj, -1)
    back = exchange(back)
    ahead = exchange(call(spread_kernel, "spread", (block,) * n_mesh, [VM] * 2, (proj, places), flops=10**8))
    base, *hots = call(
        decode_near_kernel, "decode_near",
        (shape((near_of, nodes, width), F32),) + (shape((nodes, n_mesh * count), BF),) * near_of,
        [VM] * n_mesh + [HB] * (near_of + 1), (*back, *shares, dec_source.T),
        [pltpu.VMEM((near_of, nodes), jnp.int32), pltpu.VMEM((near_of, nodes, width), BF)], flops=3 * 10**9,
    )
    grid_out = call(
        decode_kernel, "decode", pltpu.HBM(grid_latent.shape, BF), [VM] * (n_mesh + 4) + [HB] * 2,
        (*ahead, base, *hots, dec_out, grid_latent),
        [square, pltpu.VMEM((nodes, width), BF), pltpu.VMEM((nodes, width), BF)],
        flops=3 * 10**9, outs=HB, copies=4,
    )
    return (grid_out, latent)


def solution(mesh):
    placed = (
        P(("grid", "mesh"), None),
        P(("grid", "mesh"), None),
        P(("grid", "mesh")),
        P(("grid", "mesh")),
        P(None, ("grid", "mesh")),
        P(("grid", "mesh")),
        P(("grid", "mesh"), None, None, None),
        P(("grid", "mesh"), None, None),
        P(("grid", "mesh")),
        P(("grid", "mesh")),
        P(None, ("grid", "mesh")),
        P(("grid", "mesh"), None, None, None),
        P(("grid", "mesh"), None),
        P(None, None, ("grid", "mesh")),
        P(),
        P(),
        P(),
        P(),
        P(),
        P(),
    )
    return jax.shard_map(
        shards,
        mesh=mesh,
        in_specs=placed,
        out_specs=(P(("grid", "mesh"), None), P(("grid", "mesh"), None)),
        check_vma=False,
    )
```

```python
import functools

import jax
import jax.numpy as jnp
from jax import lax
from jax.experimental import pallas as pl
from jax.experimental.pallas import tpu as pltpu
from jax.sharding import PartitionSpec as P

BF = jnp.bfloat16
F32 = jnp.float32
VM = pl.BlockSpec(memory_space=pltpu.VMEM)
SM = pl.BlockSpec(memory_space=pltpu.SMEM)
HB = pl.BlockSpec(memory_space=pltpu.HBM)
ANY = pl.BlockSpec(memory_space=pl.ANY)
MIB = 1024 * 1024
BLOCK = 512
OPPOSITE = 2
EXTRA = 16
PREP = 10**10


def mm(a, b):
    return lax.dot_general(a, b, (((1,), (0,)), ((), ())), preferred_element_type=F32)


def mm_tn(a, b):
    return lax.dot_general(a, b, (((0,), (0,)), ((), ())), preferred_element_type=F32)


def to_columns(row):
    n = row.shape[1]
    parts = [jnp.broadcast_to(row[:, at:at + 128], (128, 128)).T for at in range(0, n, 128)]
    return jnp.concatenate(parts, axis=0) if len(parts) > 1 else parts[0]


def lane_hits(columns, at):
    return columns == lax.broadcasted_iota(jnp.int16, columns.shape, 1) + jnp.int16(at)


def as_ones(hits):
    return jnp.where(hits, jnp.ones(hits.shape, BF), jnp.zeros(hits.shape, BF))


def pick_matrix(columns, width, start=0):
    col = columns.astype(jnp.int16)
    return jnp.concatenate([as_ones(lane_hits(col, at)) for at in range(start, start + width, 128)], axis=1)


def add_matrix(row, height):
    n = row.shape[1]
    wide = jnp.broadcast_to(row, (16, n)).astype(jnp.int16)
    wide = jnp.broadcast_to(wide[None], (height // 16, 16, n)).reshape(height, n)
    return as_ones(wide == lax.broadcasted_iota(jnp.int16, (height, n), 0))


def split3(x):
    a = x.astype(BF).astype(F32)
    r = x - a
    b = r.astype(BF).astype(F32)
    return a, b, r - b


def lift(geometry, right):
    a, b, c = split3(geometry)
    return mm_tn(jnp.concatenate([a, a, b, b, a, c], axis=0).astype(BF), right)


def lift_right(weight):
    a, b, c = split3(weight)
    return jnp.concatenate([a, b, a, b, c, a], axis=0).astype(BF)


def half_silu(half):
    return half + half * jnp.tanh(half)


def centered(weight):
    wide = weight.astype(F32)
    return (wide - jnp.mean(wide, axis=-1, keepdims=True)).astype(BF)


def scaled(v):
    return v * lax.rsqrt(jnp.mean(v * v, axis=-1, keepdims=True) + 1e-05)


def norm(v):
    c = v - jnp.mean(v, axis=-1, keepdims=True)
    return c * lax.rsqrt(jnp.mean(c * c, axis=-1, keepdims=True) + 1e-05)


def node_update(latent, own, total, w_total, w_out):
    inner = own + mm(total.astype(BF), w_total)
    hidden = half_silu(inner * 0.5).astype(BF)
    return (latent.astype(F32) + scaled(mm(hidden, w_out))).astype(BF)


def padded(table, rows):
    return jnp.concatenate([table, jnp.zeros((rows - table.shape[0], table.shape[1]), BF)], axis=0)


def pick_rows(row, table):
    wide = -(-table.shape[0] // 128) * 128
    return mm(pick_matrix(to_columns(row), wide), padded(table, wide)).astype(BF)


def lanes(ref, at, count):
    return jnp.concatenate([ref[r:r + 1, :] for r in range(at // 128, (at + count) // 128)], axis=1)


class Held:
    def __init__(self, sems, **pairs):
        self.copies, self.refs = {}, {}
        for at, (name, (src, dst)) in enumerate(pairs.items()):
            self.refs[name] = dst
            self.copies[name] = pltpu.make_async_copy(src, dst, sems.at[at])
            self.copies[name].start()

    def __call__(self, name):
        if name in self.copies:
            self.copies.pop(name).wait()
        return self.refs[name]

    def wait(self):
        for name in list(self.copies):
            self(name)


class Sent:
    def __init__(self, sems):
        self.sems, self.copies = sems, []

    def __call__(self, src, dst):
        self.copies.append(pltpu.make_async_copy(src, dst, self.sems.at[len(self.copies)]))
        self.copies[-1].start()

    def wait(self):
        for copy in self.copies:
            copy.wait()


def turned(index, count, me):
    return lax.bitwise_and(index - me, count - 1)


def row_of(rows, at):
    out = None
    for s in range(rows.shape[0]):
        part = jnp.where(at == s, rows[s:s + 1, :], 0)
        out = part if out is None else out + part
    return out


def rows_from(rows, me):
    count = rows.shape[0]
    return jnp.concatenate([row_of(rows, lax.bitwise_and(me - dz, count - 1)) for dz in range(count)], axis=1)


def rows_to(rows, me):
    count = rows.shape[0]
    return jnp.concatenate([row_of(rows, lax.bitwise_and(me + dz, count - 1)) for dz in range(count)], axis=1)


def slot_sums(slot, part, n_mesh, message, outs):
    count = outs[0].shape[0]
    band = n_mesh * count
    me = lax.axis_index("mesh")
    local = slot - part * band
    turn = turned(lax.div(local, count), n_mesh, me) * count + lax.bitwise_and(local, count - 1)
    turn = jnp.where((local >= 0) & (local < band), turn, -1)
    total = mm(add_matrix(turn, band), message)
    for dz in range(n_mesh):
        outs[dz][...] = total[dz * count:(dz + 1) * count].astype(BF)


def encode_kernel(count_ref, grid_hbm, src_hbm, slot_hbm, geo_hbm, w_hbm, lift_hbm, message_ref, slot_out, *rest):
    outs, (grid_ref, src_ref, slot_ref, geo_ref, w0_ref, w1_ref, lift_ref, table_ref, sems) = rest[:4], rest[4:]
    nodes, edges = grid_ref.shape[0], message_ref.shape[0]
    held = Held(
        sems, grid=(grid_hbm, grid_ref), w0=(w_hbm.at[0], w0_ref), src=(src_hbm, src_ref), geo=(geo_hbm, geo_ref),
        lift=(lift_hbm, lift_ref), w1=(w_hbm.at[1], w1_ref), slot=(slot_hbm, slot_ref),
    )
    held.wait()
    table_ref[...] = (mm(grid_ref[...], w0_ref[...]) * 0.5).astype(BF)
    right = lift_right(lift_ref[...] * 0.5)
    cuts = [slice(at, at + BLOCK) for at in range(0, edges, BLOCK)]
    hidden = None
    for i in range(len(cuts) + 1):
        ahead = hidden
        if i < len(cuts):
            picks = pick_matrix(to_columns(lanes(src_ref, cuts[i].start, BLOCK)), nodes)
            hidden = half_silu(mm(picks, table_ref[...]) + lift(geo_ref[:, cuts[i]], right)).astype(BF)
        if i > 0:
            message_ref[cuts[i - 1], :] = norm(mm(ahead, w1_ref[...])).astype(BF)
    slot = lanes(slot_ref, 0, edges)
    slot = jnp.where(lax.broadcasted_iota(jnp.int32, slot.shape, 1) < count_ref[0], slot, -1)
    slot_out[...] = slot
    slot_sums(slot, 1, len(outs), message_ref[...], outs)


def near_kernel(message_ref, slot_ref, *outs):
    slot_sums(slot_ref[...], 0, len(outs), message_ref[...], outs)


def prep_kernel(_, halo_hbm, latent_hbm, w_hbm, next_hbm, *rest):
    latent_out, own_ref, wb_out, wc_out, wn_out, hot_ref, hot_hbm, halo_ref, wa_ref, wc_ref, sems, out_sems = rest
    held = Held(
        sems, halo=(halo_hbm, halo_ref), latent=(latent_hbm, latent_out), wa=(w_hbm.at[2], wa_ref), wc=(w_hbm.at[4], wc_ref),
        wb=(w_hbm.at[3], wb_out), wn=(next_hbm.at[0, 0], wn_out),
    )
    halo = held("halo")[...].astype(F32).astype(BF)
    places, owners = halo.shape
    row = lax.broadcasted_iota(jnp.int32, (places * owners, 128), 0)
    lane = lax.broadcasted_iota(jnp.int32, row.shape, 1)
    owner = jnp.where(lax.div(row, places) == lane, 1.0, 0.0).astype(BF)
    each = lax.dot_general(owner, halo, (((1,), (1,)), ((), ())), preferred_element_type=F32)
    mine = jnp.where(lax.bitwise_and(row, places - 1)[:, :places] == lane[:, :places], each, 0.0)
    column = jnp.broadcast_to(jnp.sum(mine, axis=1, keepdims=True), row.shape).astype(jnp.int32)
    hot_ref[...] = pick_matrix(column, hot_ref.shape[1])
    sent = Sent(out_sems)
    sent(hot_ref, hot_hbm)
    own_ref[...] = mm(held("latent")[...], held("wa")[...])
    wc_out[...] = centered(held("wc")[...])
    held("wb"), held("wn")
    sent.wait()


def far_kernel(*refs):
    *blocks, rows_ref, _, out_ref = refs
    rows = rows_from(rows_ref[1], lax.axis_index("mesh"))
    table = jnp.concatenate([b[...] for b in blocks], axis=0)
    out_ref[...] = mm(add_matrix(rows, out_ref.shape[0]), table).astype(BF)


def send_rows(hot_ref, table, sent_ref, sent_hbm, sems):
    table = padded(table, hot_ref.shape[1])
    sent = Sent(sems)
    step = sent_ref.shape[0] // sems.shape[0]
    for at in range(0, sent_ref.shape[0], step):
        cut = slice(at, at + step)
        sent_ref[cut, :] = mm(hot_ref[cut, :], table).astype(BF)
        sent(sent_ref.at[cut, :], sent_hbm.at[cut, :])
    sent.wait()


def first_kernel(*refs):
    *blocks, far_ref, rows_ref, latent_ref, own_ref, wb_ref, wc_ref, wn_ref, hot_ref, out_ref, sender_ref, sent_hbm, sent_ref, out_sems = refs
    rows = rows_from(rows_ref[0], lax.axis_index("mesh"))
    table = jnp.concatenate([b[...] for b in blocks], axis=0)
    total = mm(add_matrix(rows, out_ref.shape[0]), table)
    total = total + far_ref[...].astype(F32)
    latent = node_update(latent_ref[...], own_ref[...], total, wb_ref[...], wc_ref[...])
    out_ref[...] = latent
    sender = (mm(latent, wn_ref[...]) * 0.5).astype(BF)
    sender_ref[...] = sender
    send_rows(hot_ref, sender, sent_ref, sent_hbm, out_sems)


def before_kernel(latent_ref, sender_ref, src_hbm, tgt_hbm, geo_hbm, lift_hbm, w_hbm, *rest, layer, last):
    if last:
        (grid_hbm, decgeo_hbm, declift_hbm, dec_hbm, decsrc_hbm, rows_ref), rest = rest[:6], rest[6:]
        (*shares, decw_out, deccol_out, rowcol_out), rest = rest[:6], rest[6:]
    own_ref, src_ref, tgt_ref, *bases = rest[:5]
    (wc_out, wf_out), rest = rest[5:7], rest[7:]
    if last:
        (grid_ref, decgeo_ref, declift_ref, decv_ref, decw_ref, total_ref, share_ref, decsrc_ref, deccol_ref, rowcol_ref), rest = rest[:10], rest[10:]
    geo_ref, lift_ref, wb_ref, wd_ref, wc_ref, wf_ref, sems, out_sems = rest
    more = {}
    if last:
        more = dict(
            grid=(grid_hbm, grid_ref), decgeo=(decgeo_hbm, decgeo_ref), declift=(declift_hbm, declift_ref),
            decv=(dec_hbm.at[1], decv_ref), decw=(dec_hbm.at[2], decw_ref), decsrc=(decsrc_hbm, decsrc_ref),
        )
    held = Held(
        sems, wb=(w_hbm.at[layer, 1], wb_ref), src=(src_hbm, src_ref), tgt=(tgt_hbm, tgt_ref), geo=(geo_hbm, geo_ref),
        lift=(lift_hbm.at[layer], lift_ref), wd=(w_hbm.at[layer, 3], wd_ref), wc=(w_hbm.at[layer, 2], wc_ref),
        wf=(w_hbm.at[layer, 5], wf_ref), **more,
    )
    sent = Sent(out_sems)
    latent = latent_ref[...]
    rows = latent.shape[0]
    target = (mm(latent, held("wb")[...]) * 0.5).astype(BF)
    wide = -(-2 * rows // 128) * 128
    table = padded(jnp.concatenate([sender_ref[...], target], axis=0), wide)
    held("src"), held("tgt"), held("geo")
    right = lift_right(held("lift")[...] * 0.5)
    for part, base_ref in enumerate(bases):
        for at in range(0, base_ref.shape[0], 128):
            near = part * base_ref.shape[0] + at
            src = to_columns(lanes(src_ref, near, 128))
            src_col = jnp.where(src < rows, src, -1).astype(jnp.int16)
            tgt_col = to_columns(lanes(tgt_ref, near, 128) + rows).astype(jnp.int16)
            groups = [as_ones(lane_hits(src_col, lane) | lane_hits(tgt_col, lane)) for lane in range(0, wide, 128)]
            base = mm(jnp.concatenate(groups, axis=1), table) + lift(geo_ref[:, near:near + 128], right)
            base_ref[at:at + 128, :] = base.astype(BF)
    own_ref[...] = mm(latent, held("wd")[...]).astype(BF)
    wc_ref[...] = centered(held("wc")[...])
    sent(wc_ref, wc_out)
    wf_ref[...] = centered(held("wf")[...])
    sent(wf_ref, wf_out)
    if last:
        right = lift_right(held("declift")[...] * 0.5)
        total_ref[...] = mm(held("grid")[...], held("decv")[...]) * 0.5
        decw_ref[...] = centered(held("decw")[...])
        sent(decw_ref, decw_out)
        n_mesh, count = rows_ref.shape[1:]
        rowcol_ref[...] = to_columns(rows_to(rows_ref[0], lax.axis_index("mesh"))).astype(jnp.int16)
        sent(rowcol_ref, rowcol_out)
        held("decsrc")
        for which in range(decsrc_ref.shape[0]):
            deccol_ref[which] = place_columns(decsrc_ref[which:which + 1, :], n_mesh, count).astype(jnp.int16)
            sent(deccol_ref.at[which], deccol_out.at[which])
        held("decgeo")
        for which, out in enumerate(shares):
            for at in range(0, out.shape[0], 256):
                cut = slice(at, at + 256)
                share_ref[which, cut, :] = (lift(decgeo_ref[which, :, cut], right) + total_ref[cut, :]).astype(BF)
            sent(share_ref.at[which], out)
    sent.wait()


def layer_kernel(latent_ref, came_ref, own_ref, src_ref, tgt_ref, *rest, layer, last):
    (*bases, wc_hbm, wf_hbm, w_hbm, next_hbm, pick_ref, places_ref), rest = rest[:8], rest[8:]
    outs, (message_ref, wc_ref, we_ref, wf_ref, wn_ref, hot_ref, sent_ref, sems, out_sems) = rest[:-9], rest[-9:]
    held = Held(
        sems, wc=(wc_hbm, wc_ref), we=(w_hbm.at[layer, 4], we_ref), wf=(wf_hbm, wf_ref),
        wn=(next_hbm.at[0] if last else next_hbm.at[layer + 1, 0], wn_ref), **({} if last else dict(hot=(pick_ref, hot_ref))),
    )
    rows = latent_ref.shape[0]
    for part, base_ref in enumerate(bases):
        count = base_ref.shape[0]
        cut = slice(part * count, (part + 1) * count)
        columns = to_columns(lanes(src_ref, part * count, count)) - rows
        half = mm(pick_matrix(columns, came_ref.shape[0]), came_ref[...]) + base_ref[...].astype(F32)
        message_ref[cut, :] = scaled(mm(half_silu(half).astype(BF), held("wc")[...])).astype(BF)
    total = mm(add_matrix(lanes(tgt_ref, 0, message_ref.shape[0]), rows), message_ref[...])
    latent = node_update(latent_ref[...], own_ref[...].astype(F32), total, held("we")[...], held("wf")[...])
    outs[0][...] = latent
    onward = mm(latent, held("wn")[...])
    if last:
        onward = onward.astype(BF)
        outs[1][:rows, :] = onward
        places = jnp.concatenate([places_ref[1, m:m + 1, :] for m in range(places_ref.shape[1])], axis=1).astype(F32)
        outs[1][rows:, :] = jnp.broadcast_to(places, (outs[1].shape[0] - rows, places.shape[1])).astype(BF)
        spread(to_columns(rows_to(places_ref[0], lax.axis_index("mesh"))), onward, outs[2:])
    else:
        onward = (onward * 0.5).astype(BF)
        outs[1][...] = onward
        send_rows(held("hot"), onward, sent_ref, outs[2], out_sems)


def spread(columns, table, outs):
    wide = -(-table.shape[0] // 128) * 128
    picked = mm(pick_matrix(columns, wide), padded(table, wide)).astype(BF)
    count = outs[0].shape[0]
    for dz, out in enumerate(outs):
        out[out.shape[0] - count:, :] = picked[dz * count:(dz + 1) * count]


def spread_kernel(moved_ref, opposite_ref, *outs):
    rows = moved_ref.shape[0] - EXTRA
    count = outs[0].shape[0]
    places = moved_ref[rows:rows + 16, :].astype(F32).astype(jnp.int32)[:1, :]
    places = jnp.concatenate([places[:, m * count:(m + 1) * count] for m in range(len(outs))], axis=0)
    outs[OPPOSITE][:count, :] = opposite_ref[...]
    spread(to_columns(rows_to(places, lax.axis_index("mesh"))), moved_ref[:rows, :], outs)


def place_columns(place, n_mesh, count):
    me = lax.axis_index("mesh")
    block = lax.div(place, count)
    turn = lax.bitwise_and(me - block, n_mesh - 1) + lax.bitwise_and(block, -n_mesh)
    turn = jnp.where(turn == OPPOSITE, n_mesh - 1, jnp.where(turn == n_mesh - 1, OPPOSITE, turn))
    return to_columns(turn * count + lax.bitwise_and(place, count - 1))


def decode_near_kernel(*refs):
    *blocks, dec0, dec1, dec2, col_hbm, base_ref, hot0, hot1, hot2, col_ref, share_ref, sems = refs
    held = Held(sems, **{
        name: pair for i, dec in enumerate((dec0, dec1, dec2))
        for name, pair in ((f"c{i}", (col_hbm.at[i], col_ref.at[i])), (f"d{i}", (dec, share_ref.at[i])))
    })
    table = jnp.concatenate([b[...] for b in blocks], axis=0) * 0.5
    width, rest = table.shape[0], hot0.shape[1]
    for which, hot in enumerate((hot0, hot1, hot2)):
        held(f"c{which}"), held(f"d{which}")
        for at in range(0, base_ref.shape[1], BLOCK):
            cut = slice(at, at + BLOCK)
            column = col_ref[which, cut, :]
            base_ref[which, cut, :] = mm(pick_matrix(column, width), table) + share_ref[which, cut, :].astype(F32)
            hot[cut, :] = pick_matrix(column, rest, width)


def decode_kernel(*refs):
    *blocks, base_ref, hot0, hot1, hot2, w_hbm, grid_hbm, out_hbm, w_ref, grid_ref, out_ref, sems, out_sems = refs
    held = Held(sems, w=(w_hbm, w_ref), grid=(grid_hbm, grid_ref))
    count = blocks[0].shape[0]
    table = [blocks[OPPOSITE][:count, :]] + [b[b.shape[0] - count:, :] for b in blocks]
    table = jnp.concatenate(table, axis=0) * 0.5
    step = out_ref.shape[0] // out_sems.shape[0]
    sent = []
    for at in range(0, out_ref.shape[0], step):
        cut = slice(at, at + step)
        hidden = None
        for which, hot in enumerate((hot0, hot1, hot2)):
            more = half_silu(base_ref[which, cut, :] + mm(hot[cut, :], table))
            hidden = more if hidden is None else hidden + more
        update = scaled(mm(hidden.astype(BF), held("w")[...]))
        out_ref[cut, :] = (held("grid")[cut, :].astype(F32) + update).astype(BF)
        sent.append(pltpu.make_async_copy(out_ref.at[cut, :], out_hbm.at[cut, :], out_sems.at[at // step]))
        sent[-1].start()
    for copy in sent:
        copy.wait()


def call(kernel, name, out, specs, args, scratch=(), flops=0, limit=24, outs=None, copies=0, wait=True):
    if scratch and wait:
        scratch = list(scratch) + [pltpu.SemaphoreType.DMA((16,))]
    if copies:
        scratch.append(pltpu.SemaphoreType.DMA((copies,)))
    args = [pltpu.with_memory_space_constraint(a, pltpu.HBM) if s is HB else a for s, a in zip(specs, args)]
    return pl.pallas_call(
        kernel,
        out_shape=out,
        in_specs=specs,
        out_specs=jax.tree.map(lambda _: VM, out) if outs is None else outs,
        scratch_shapes=scratch,
        compiler_params=pltpu.CompilerParams(vmem_limit_bytes=limit * MIB),
        cost_estimate=pl.CostEstimate(flops=flops, bytes_accessed=4 * MIB, transcendentals=0),
        name=name,
    )(*args)


def strip_shift(value, by):
    length = lax.axis_size("grid")
    pairs = [(i, i + by) for i in range(length) if 0 <= i + by < length]
    return lax.ppermute(value, "grid", pairs)


def exchange(blocks, steps=None):
    length = lax.axis_size("mesh")
    moved = []
    for dz, block in zip(steps or range(length), blocks):
        pairs = [(i, (i + dz) % length) for i in range(length)]
        moved.append(lax.ppermute(block, "mesh", pairs) if dz else block)
    return moved


def shards(
    grid_latent,
    mesh_latent,
    enc_source,
    enc_slot,
    enc_geometry,
    edge_count,
    slot_row,
    halo_rows,
    proc_source,
    proc_target,
    proc_geometry,
    return_rows,
    dec_source,
    dec_geometry,
    enc_weights,
    enc_lift,
    proc_weights,
    proc_lift,
    dec_weights,
    dec_lift,
):
    nodes, width = grid_latent.shape
    mesh_rows = mesh_latent.shape[0]
    n_mesh = lax.axis_size("mesh")
    count = slot_row.shape[3]
    edges, links = enc_source.shape[0], proc_source.shape[0]
    near_of = dec_source.shape[1]
    shape = jax.ShapeDtypeStruct
    block = shape((count, width), BF)
    row = shape((mesh_rows, width), BF)
    wide_row = shape((mesh_rows, width), F32)
    weight = shape((width, width), BF)
    square = pltpu.VMEM((width, width), BF)
    lifts = pltpu.VMEM(enc_lift.shape, F32)
    above = strip_shift(slot_row[0], -1)
    message, slot, *far = call(
        encode_kernel, "encode", (shape((edges, width), BF), shape((1, edges), jnp.int32)) + (block,) * n_mesh, [SM] + [HB] * 6,
        (edge_count, grid_latent, enc_source.reshape(-1, 128), enc_slot.reshape(-1, 128), enc_geometry, enc_weights, enc_lift),
        [pltpu.VMEM((nodes, width), BF), pltpu.VMEM((edges // 128, 128), jnp.int32),
         pltpu.VMEM((edges // 128, 128), jnp.int32), pltpu.VMEM((4, edges), F32), square, square, lifts,
         pltpu.VMEM((nodes, width), BF)],
        flops=5 * 10**9,
    )
    far = exchange(far)
    halo = halo_rows[0].T
    sends = pltpu.HBM((halo.size, width), BF)
    sending = pltpu.VMEM((halo.size, width), BF)
    hot = shape((halo.size, -(-mesh_rows // 128) * 128), BF)
    near = call(near_kernel, "near", (block,) * n_mesh, [VM] * 2, (message, slot), flops=10**9)
    up = call(far_kernel, "far", (row,), [VM] * (n_mesh + 1) + [ANY], (*far, above, near[0]), flops=10**8)
    near = exchange(near)
    start, own, wb, wc, wn, hot, hot_far = call(
        prep_kernel, "prep", (row, wide_row, weight, weight, weight, hot, pltpu.HBM(hot.shape, BF)),
        [ANY] + [HB] * 4, (up[0], halo, mesh_latent, enc_weights, proc_weights),
        [pltpu.VMEM(halo.shape, jnp.int32), square, square], flops=PREP, outs=(VM,) * 6 + (HB,), copies=1,
    )
    up = strip_shift(up[0], 1)
    latent, sender, sent = call(
        first_kernel, "first", (row, row, sends), [VM] * (n_mesh + 8),
        (*near, up, slot_row[0], start, own, wb, wc, wn, hot), [sending], flops=10**9, outs=(VM, VM, HB), copies=4, wait=False,
    )
    layers = proc_weights.shape[0]
    moved = shape((mesh_rows + EXTRA, width), BF)
    half = shape((links // 2, width), BF)
    index = shape((links // 128, 128), jnp.int32)
    for layer in range(layers):
        came = lax.all_to_all(
            sent.reshape(lax.axis_size("grid") * n_mesh, -1, width), ("grid", "mesh"), split_axis=0, concat_axis=0, tiled=True
        ).reshape(sent.shape)
        last = layer + 1 == layers
        operands = [
            latent, sender, proc_source.reshape(-1, 128), proc_target.reshape(-1, 128), proc_geometry, proc_lift, proc_weights,
        ]
        outs = (row, index, index, half, half) + (pltpu.HBM(weight.shape, BF),) * 2
        out_specs = (VM,) * 5 + (HB,) * 2
        scratch = [pltpu.VMEM((4, links), F32), lifts, square, square, square, square]
        specs = [VM] * 2 + [HB] * 5
        if last:
            operands += [grid_latent, dec_geometry.transpose(1, 0, 2), dec_lift, dec_weights, dec_source.T, return_rows[0]]
            specs += [HB] * 5 + [VM]
            outs = (pltpu.HBM((nodes, width), BF),) * near_of + (
                pltpu.HBM(weight.shape, BF), pltpu.HBM((near_of, nodes, 128), jnp.int16), pltpu.HBM((n_mesh * count, 128), jnp.int16),
            ) + outs
            out_specs = (HB,) * (near_of + 3) + out_specs
            scratch = [
                pltpu.VMEM((nodes, width), BF), pltpu.VMEM((near_of, 4, nodes), F32), lifts, square, square,
                pltpu.VMEM((nodes, width), F32), pltpu.VMEM((near_of, nodes, width), BF), pltpu.VMEM((near_of, nodes), jnp.int32),
                pltpu.VMEM((near_of, nodes, 128), jnp.int16), pltpu.VMEM((n_mesh * count, 128), jnp.int16),
            ] + scratch
        held = list(call(
            functools.partial(before_kernel, layer=layer, last=last), "before", outs, specs, operands, scratch, flops=10**9,
            outs=out_specs, copies=4 + 2 * near_of,
        ))
        if last:
            *shares, dec_out, places_out, rows_out = held[:near_of + 3]
            held = held[near_of + 3:]
        out = call(
            functools.partial(layer_kernel, layer=layer, last=last), "layer",
            (row, moved) + (block,) * n_mesh if last else (row, row, sends), [VM] * 7 + [HB] * 5 + [VM],
            (latent, came, *held, proc_weights, dec_weights if last else proc_weights, rows_out if last else hot_far, return_rows[0]),
            [pltpu.VMEM((links, width), BF)] + [square] * 4
            + [pltpu.VMEM((n_mesh * count, 128), jnp.int16) if last else pltpu.VMEM(hot.shape, BF), sending], flops=4 * 10**9,
            outs=(VM,) * (2 + n_mesh) if last else (VM, VM, HB), copies=4,
        )
        if last:
            latent, proj, *back = out
        else:
            latent, sender, sent = out
    proj = strip_shift(proj, -1)
    opposite = back.pop(OPPOSITE)
    back = exchange(back, (0, 1, 3))
    ahead = call(
        spread_kernel, "spread", tuple(shape((2 * count if dz == OPPOSITE else count, width), BF) for dz in range(n_mesh)), [VM] * 2,
        (proj, opposite), flops=10**8,
    )
    ahead = exchange(ahead)
    base, *hots = call(
        decode_near_kernel, "decode_near",
        (shape((near_of, nodes, width), F32),) + (shape((nodes, (n_mesh + 1) * count), BF),) * near_of,
        [VM] * (n_mesh - 1) + [HB] * (near_of + 1), (*back, *shares, places_out),
        [pltpu.VMEM((near_of, nodes, 128), jnp.int16), pltpu.VMEM((near_of, nodes, width), BF)], flops=3 * 10**9,
    )
    grid_out = call(
        decode_kernel, "decode", pltpu.HBM(grid_latent.shape, BF), [VM] * (n_mesh + 4) + [HB] * 2,
        (*ahead, base, *hots, dec_out, grid_latent),
        [square, pltpu.VMEM((nodes, width), BF), pltpu.VMEM((nodes, width), BF)],
        flops=3 * 10**9, outs=HB, copies=4,
    )
    return (grid_out, latent)


def solution(mesh):
    placed = (
        P(("grid", "mesh"), None),
        P(("grid", "mesh"), None),
        P(("grid", "mesh")),
        P(("grid", "mesh")),
        P(None, ("grid", "mesh")),
        P(("grid", "mesh")),
        P(("grid", "mesh"), None, None, None),
        P(("grid", "mesh"), None, None),
        P(("grid", "mesh")),
        P(("grid", "mesh")),
        P(None, ("grid", "mesh")),
        P(("grid", "mesh"), None, None, None),
        P(("grid", "mesh"), None),
        P(None, None, ("grid", "mesh")),
        P(),
        P(),
        P(),
        P(),
        P(),
        P(),
    )
    return jax.shard_map(
        shards,
        mesh=mesh,
        in_specs=placed,
        out_specs=(P(("grid", "mesh"), None), P(("grid", "mesh"), None)),
        check_vma=False,
    )
```

```python
import functools

import jax
import jax.numpy as jnp
from jax import lax
from jax.experimental import pallas as pl
from jax.experimental.pallas import tpu as pltpu
from jax.sharding import PartitionSpec as P

BF = jnp.bfloat16
F32 = jnp.float32
VM = pl.BlockSpec(memory_space=pltpu.VMEM)
SM = pl.BlockSpec(memory_space=pltpu.SMEM)
HB = pl.BlockSpec(memory_space=pltpu.HBM)
ANY = pl.BlockSpec(memory_space=pl.ANY)
MIB = 1024 * 1024
BLOCK = 512
RIDING = 3
EXTRA = 16
PREP = 10**10


def mm(a, b):
    return lax.dot_general(a, b, (((1,), (0,)), ((), ())), preferred_element_type=F32)


def mm_tn(a, b):
    return lax.dot_general(a, b, (((0,), (0,)), ((), ())), preferred_element_type=F32)


def to_columns(row):
    n = row.shape[1]
    parts = [jnp.broadcast_to(row[:, at:at + 128], (128, 128)).T for at in range(0, n, 128)]
    return jnp.concatenate(parts, axis=0) if len(parts) > 1 else parts[0]


def lane_hits(columns, at):
    return columns == lax.broadcasted_iota(jnp.int16, columns.shape, 1) + jnp.int16(at)


def as_ones(hits):
    return jnp.where(hits, jnp.ones(hits.shape, BF), jnp.zeros(hits.shape, BF))


def pick_matrix(columns, width, start=0):
    col = columns.astype(jnp.int16)
    return jnp.concatenate([as_ones(lane_hits(col, at)) for at in range(start, start + width, 128)], axis=1)


def add_matrix(row, height):
    n = row.shape[1]
    wide = jnp.broadcast_to(row, (16, n)).astype(jnp.int16)
    wide = jnp.broadcast_to(wide[None], (height // 16, 16, n)).reshape(height, n)
    return as_ones(wide == lax.broadcasted_iota(jnp.int16, (height, n), 0))


def split3(x):
    a = x.astype(BF).astype(F32)
    r = x - a
    b = r.astype(BF).astype(F32)
    return a, b, r - b


def lift(geometry, right):
    a, b, c = split3(geometry)
    return mm_tn(jnp.concatenate([a, a, b, b, a, c], axis=0).astype(BF), right)


def lift_right(weight):
    a, b, c = split3(weight)
    return jnp.concatenate([a, b, a, b, c, a], axis=0).astype(BF)


def half_silu(half):
    return half + half * jnp.tanh(half)


def centered(weight):
    wide = weight.astype(F32)
    return (wide - jnp.mean(wide, axis=-1, keepdims=True)).astype(BF)


def scaled(v):
    return v * lax.rsqrt(jnp.mean(v * v, axis=-1, keepdims=True) + 1e-05)


def norm(v):
    c = v - jnp.mean(v, axis=-1, keepdims=True)
    return c * lax.rsqrt(jnp.mean(c * c, axis=-1, keepdims=True) + 1e-05)


def node_update(latent, own, total, w_total, w_out):
    inner = own + mm(total.astype(BF), w_total)
    hidden = half_silu(inner * 0.5).astype(BF)
    return (latent.astype(F32) + scaled(mm(hidden, w_out))).astype(BF)


def padded(table, rows):
    return jnp.concatenate([table, jnp.zeros((rows - table.shape[0], table.shape[1]), BF)], axis=0)


def pick_rows(row, table):
    wide = -(-table.shape[0] // 128) * 128
    return mm(pick_matrix(to_columns(row), wide), padded(table, wide)).astype(BF)


def lanes(ref, at, count):
    return jnp.concatenate([ref[r:r + 1, :] for r in range(at // 128, (at + count) // 128)], axis=1)


class Held:
    def __init__(self, sems, **pairs):
        self.copies, self.refs = {}, {}
        for at, (name, (src, dst)) in enumerate(pairs.items()):
            self.refs[name] = dst
            self.copies[name] = pltpu.make_async_copy(src, dst, sems.at[at])
            self.copies[name].start()

    def __call__(self, name):
        if name in self.copies:
            self.copies.pop(name).wait()
        return self.refs[name]

    def wait(self):
        for name in list(self.copies):
            self(name)


class Sent:
    def __init__(self, sems):
        self.sems, self.copies = sems, []

    def __call__(self, src, dst):
        self.copies.append(pltpu.make_async_copy(src, dst, self.sems.at[len(self.copies)]))
        self.copies[-1].start()

    def wait(self):
        for copy in self.copies:
            copy.wait()


def turned(index, count, me):
    return lax.bitwise_and(index - me, count - 1)


def row_of(rows, at):
    out = None
    for s in range(rows.shape[0]):
        part = jnp.where(at == s, rows[s:s + 1, :], 0)
        out = part if out is None else out + part
    return out


def rows_from(rows, me):
    count = rows.shape[0]
    return jnp.concatenate([row_of(rows, lax.bitwise_and(me - dz, count - 1)) for dz in range(count)], axis=1)


def rows_to(rows, me):
    count = rows.shape[0]
    return jnp.concatenate([row_of(rows, lax.bitwise_and(me + dz, count - 1)) for dz in range(count)], axis=1)


def slot_sums(slot, part, n_mesh, message, outs):
    count = outs[0].shape[0]
    band = n_mesh * count
    me = lax.axis_index("mesh")
    local = slot - part * band
    turn = turned(lax.div(local, count), n_mesh, me) * count + lax.bitwise_and(local, count - 1)
    turn = jnp.where((local >= 0) & (local < band), turn, -1)
    total = mm(add_matrix(turn, band), message)
    for dz in range(n_mesh):
        outs[dz][...] = total[dz * count:(dz + 1) * count].astype(BF)


def encode_kernel(count_ref, grid_hbm, src_hbm, slot_hbm, geo_hbm, w_hbm, lift_hbm, message_ref, slot_out, *rest):
    outs, (grid_ref, src_ref, slot_ref, geo_ref, w0_ref, w1_ref, lift_ref, table_ref, sems) = rest[:4], rest[4:]
    nodes, edges = grid_ref.shape[0], message_ref.shape[0]
    held = Held(
        sems, grid=(grid_hbm, grid_ref), w0=(w_hbm.at[0], w0_ref), src=(src_hbm, src_ref), geo=(geo_hbm, geo_ref),
        lift=(lift_hbm, lift_ref), w1=(w_hbm.at[1], w1_ref), slot=(slot_hbm, slot_ref),
    )
    held.wait()
    table_ref[...] = (mm(grid_ref[...], w0_ref[...]) * 0.5).astype(BF)
    right = lift_right(lift_ref[...] * 0.5)
    cuts = [slice(at, at + BLOCK) for at in range(0, edges, BLOCK)]
    hidden = None
    for i in range(len(cuts) + 1):
        ahead = hidden
        if i < len(cuts):
            picks = pick_matrix(to_columns(lanes(src_ref, cuts[i].start, BLOCK)), nodes)
            hidden = half_silu(mm(picks, table_ref[...]) + lift(geo_ref[:, cuts[i]], right)).astype(BF)
        if i > 0:
            message_ref[cuts[i - 1], :] = norm(mm(ahead, w1_ref[...])).astype(BF)
    slot = lanes(slot_ref, 0, edges)
    slot = jnp.where(lax.broadcasted_iota(jnp.int32, slot.shape, 1) < count_ref[0], slot, -1)
    slot_out[...] = slot
    slot_sums(slot, 1, len(outs), message_ref[...], outs)


def near_kernel(message_ref, slot_ref, *outs):
    slot_sums(slot_ref[...], 0, len(outs), message_ref[...], outs)


def prep_kernel(_, halo_hbm, latent_hbm, w_hbm, next_hbm, *rest):
    latent_out, own_ref, wb_out, wc_out, wn_out, hot_ref, hot_hbm, halo_ref, wa_ref, wc_ref, sems, out_sems = rest
    held = Held(
        sems, halo=(halo_hbm, halo_ref), latent=(latent_hbm, latent_out), wa=(w_hbm.at[2], wa_ref), wc=(w_hbm.at[4], wc_ref),
        wb=(w_hbm.at[3], wb_out), wn=(next_hbm.at[0, 0], wn_out),
    )
    halo = held("halo")[...].astype(F32).astype(BF)
    places, owners = halo.shape
    row = lax.broadcasted_iota(jnp.int32, (places * owners, 128), 0)
    lane = lax.broadcasted_iota(jnp.int32, row.shape, 1)
    owner = jnp.where(lax.div(row, places) == lane, 1.0, 0.0).astype(BF)
    each = lax.dot_general(owner, halo, (((1,), (1,)), ((), ())), preferred_element_type=F32)
    mine = jnp.where(lax.bitwise_and(row, places - 1)[:, :places] == lane[:, :places], each, 0.0)
    column = jnp.broadcast_to(jnp.sum(mine, axis=1, keepdims=True), row.shape).astype(jnp.int32)
    hot_ref[...] = pick_matrix(column, hot_ref.shape[1])
    sent = Sent(out_sems)
    sent(hot_ref, hot_hbm)
    own_ref[...] = mm(held("latent")[...], held("wa")[...])
    wc_out[...] = centered(held("wc")[...])
    held("wb"), held("wn")
    sent.wait()


def far_kernel(*refs):
    *blocks, rows_ref, _, out_ref = refs
    rows = rows_from(rows_ref[1], lax.axis_index("mesh"))
    table = jnp.concatenate([b[...] for b in blocks], axis=0)
    out_ref[...] = mm(add_matrix(rows, out_ref.shape[0]), table).astype(BF)


def send_rows(hot_ref, table, sent_ref, sent_hbm, sems):
    table = padded(table, hot_ref.shape[1])
    sent = Sent(sems)
    step = sent_ref.shape[0] // sems.shape[0]
    for at in range(0, sent_ref.shape[0], step):
        cut = slice(at, at + step)
        sent_ref[cut, :] = mm(hot_ref[cut, :], table).astype(BF)
        sent(sent_ref.at[cut, :], sent_hbm.at[cut, :])
    sent.wait()


def first_kernel(*refs):
    *blocks, far_ref, rows_ref, latent_ref, own_ref, wb_ref, wc_ref, wn_ref, hot_ref, out_ref, sender_ref, sent_hbm, sent_ref, out_sems = refs
    rows = rows_from(rows_ref[0], lax.axis_index("mesh"))
    table = jnp.concatenate([b[...] for b in blocks], axis=0)
    total = mm(add_matrix(rows, out_ref.shape[0]), table)
    total = total + far_ref[...].astype(F32)
    latent = node_update(latent_ref[...], own_ref[...], total, wb_ref[...], wc_ref[...])
    out_ref[...] = latent
    sender = (mm(latent, wn_ref[...]) * 0.5).astype(BF)
    sender_ref[...] = sender
    send_rows(hot_ref, sender, sent_ref, sent_hbm, out_sems)


def before_kernel(latent_ref, sender_ref, src_hbm, tgt_hbm, geo_hbm, lift_hbm, w_hbm, *rest, layer, last):
    if last:
        (grid_hbm, decgeo_hbm, declift_hbm, dec_hbm, decsrc_hbm, rows_ref), rest = rest[:6], rest[6:]
        (*shares, decw_out, deccol_out, rowcol_out), rest = rest[:6], rest[6:]
    own_ref, src_ref, tgt_ref, *bases = rest[:5]
    (wc_out, wf_out), rest = rest[5:7], rest[7:]
    if last:
        (grid_ref, decgeo_ref, declift_ref, decv_ref, decw_ref, total_ref, share_ref, decsrc_ref, deccol_ref, rowcol_ref), rest = rest[:10], rest[10:]
    geo_ref, lift_ref, wb_ref, wd_ref, wc_ref, wf_ref, sems, out_sems = rest
    more = {}
    if last:
        more = dict(
            grid=(grid_hbm, grid_ref), decgeo=(decgeo_hbm, decgeo_ref), declift=(declift_hbm, declift_ref),
            decv=(dec_hbm.at[1], decv_ref), decw=(dec_hbm.at[2], decw_ref), decsrc=(decsrc_hbm, decsrc_ref),
        )
    held = Held(
        sems, wb=(w_hbm.at[layer, 1], wb_ref), src=(src_hbm, src_ref), tgt=(tgt_hbm, tgt_ref), geo=(geo_hbm, geo_ref),
        lift=(lift_hbm.at[layer], lift_ref), wd=(w_hbm.at[layer, 3], wd_ref), wc=(w_hbm.at[layer, 2], wc_ref),
        wf=(w_hbm.at[layer, 5], wf_ref), **more,
    )
    sent = Sent(out_sems)
    latent = latent_ref[...]
    rows = latent.shape[0]
    target = (mm(latent, held("wb")[...]) * 0.5).astype(BF)
    wide = -(-2 * rows // 128) * 128
    table = padded(jnp.concatenate([sender_ref[...], target], axis=0), wide)
    held("src"), held("tgt"), held("geo")
    right = lift_right(held("lift")[...] * 0.5)
    for part, base_ref in enumerate(bases):
        for at in range(0, base_ref.shape[0], 128):
            near = part * base_ref.shape[0] + at
            src = to_columns(lanes(src_ref, near, 128))
            src_col = jnp.where(src < rows, src, -1).astype(jnp.int16)
            tgt_col = to_columns(lanes(tgt_ref, near, 128) + rows).astype(jnp.int16)
            groups = [as_ones(lane_hits(src_col, lane) | lane_hits(tgt_col, lane)) for lane in range(0, wide, 128)]
            base = mm(jnp.concatenate(groups, axis=1), table) + lift(geo_ref[:, near:near + 128], right)
            base_ref[at:at + 128, :] = base.astype(BF)
    own_ref[...] = mm(latent, held("wd")[...]).astype(BF)
    wc_ref[...] = centered(held("wc")[...])
    sent(wc_ref, wc_out)
    wf_ref[...] = centered(held("wf")[...])
    sent(wf_ref, wf_out)
    if last:
        right = lift_right(held("declift")[...] * 0.5)
        total_ref[...] = mm(held("grid")[...], held("decv")[...]) * 0.5
        decw_ref[...] = centered(held("decw")[...])
        sent(decw_ref, decw_out)
        n_mesh, count = rows_ref.shape[1:]
        rowcol_ref[...] = to_columns(rows_to(rows_ref[0], lax.axis_index("mesh"))).astype(jnp.int16)
        sent(rowcol_ref, rowcol_out)
        held("decsrc")
        for which in range(decsrc_ref.shape[0]):
            deccol_ref[which] = place_columns(decsrc_ref[which:which + 1, :], n_mesh, count).astype(jnp.int16)
            sent(deccol_ref.at[which], deccol_out.at[which])
        held("decgeo")
        for which, out in enumerate(shares):
            for at in range(0, out.shape[0], 256):
                cut = slice(at, at + 256)
                share_ref[which, cut, :] = (lift(decgeo_ref[which, :, cut], right) + total_ref[cut, :]).astype(BF)
            sent(share_ref.at[which], out)
    sent.wait()


def layer_kernel(latent_ref, came_ref, own_ref, src_ref, tgt_ref, *rest, layer, last):
    (*bases, wc_hbm, wf_hbm, w_hbm, next_hbm, pick_ref, places_ref), rest = rest[:8], rest[8:]
    outs, (message_ref, wc_ref, we_ref, wf_ref, wn_ref, hot_ref, sent_ref, sems, out_sems) = rest[:-9], rest[-9:]
    held = Held(
        sems, wc=(wc_hbm, wc_ref), we=(w_hbm.at[layer, 4], we_ref), wf=(wf_hbm, wf_ref),
        wn=(next_hbm.at[0] if last else next_hbm.at[layer + 1, 0], wn_ref), **({} if last else dict(hot=(pick_ref, hot_ref))),
    )
    rows = latent_ref.shape[0]
    for part, base_ref in enumerate(bases):
        count = base_ref.shape[0]
        cut = slice(part * count, (part + 1) * count)
        columns = to_columns(lanes(src_ref, part * count, count)) - rows
        half = mm(pick_matrix(columns, came_ref.shape[0]), came_ref[...]) + base_ref[...].astype(F32)
        message_ref[cut, :] = scaled(mm(half_silu(half).astype(BF), held("wc")[...])).astype(BF)
    total = mm(add_matrix(lanes(tgt_ref, 0, message_ref.shape[0]), rows), message_ref[...])
    latent = node_update(latent_ref[...], own_ref[...].astype(F32), total, held("we")[...], held("wf")[...])
    outs[0][...] = latent
    onward = mm(latent, held("wn")[...])
    if last:
        onward = onward.astype(BF)
        outs[1][:rows, :] = onward
        places = jnp.concatenate([places_ref[1, m:m + 1, :] for m in range(places_ref.shape[1])], axis=1).astype(F32)
        outs[1][rows:, :] = jnp.broadcast_to(places, (outs[1].shape[0] - rows, places.shape[1])).astype(BF)
        spread(to_columns(rows_to(places_ref[0], lax.axis_index("mesh"))), onward, outs[2:])
    else:
        onward = (onward * 0.5).astype(BF)
        outs[1][...] = onward
        send_rows(held("hot"), onward, sent_ref, outs[2], out_sems)


def spread(columns, table, outs):
    wide = -(-table.shape[0] // 128) * 128
    picked = mm(pick_matrix(columns, wide), padded(table, wide)).astype(BF)
    count = outs[0].shape[0]
    for dz, out in enumerate(outs):
        out[out.shape[0] - count:, :] = picked[dz * count:(dz + 1) * count]


def spread_kernel(moved_ref, riding_ref, *outs):
    rows = moved_ref.shape[0] - EXTRA
    count = outs[0].shape[0]
    places = moved_ref[rows:rows + 16, :].astype(F32).astype(jnp.int32)[:1, :]
    places = jnp.concatenate([places[:, m * count:(m + 1) * count] for m in range(len(outs))], axis=0)
    outs[RIDING][:count, :] = riding_ref[...]
    spread(to_columns(rows_to(places, lax.axis_index("mesh"))), moved_ref[:rows, :], outs)


def place_columns(place, n_mesh, count):
    me = lax.axis_index("mesh")
    block = lax.div(place, count)
    turn = lax.bitwise_and(me - block, n_mesh - 1) + lax.bitwise_and(block, -n_mesh)
    turn = jnp.where(turn == RIDING, n_mesh, jnp.where((turn > RIDING) & (turn <= n_mesh), turn - 1, turn))
    return to_columns(turn * count + lax.bitwise_and(place, count - 1))


def decode_near_kernel(*refs):
    *blocks, dec0, dec1, dec2, col_hbm, w_hbm, grid_hbm, base_ref, hot0, hot1, hot2, w_out, grid_out, col_ref, share_ref, sems = refs
    pairs = {}
    for i, dec in enumerate((dec0, dec1, dec2)):
        pairs.update({f"c{i}": (col_hbm.at[i], col_ref.at[i]), f"d{i}": (dec, share_ref.at[i])})
    held = Held(sems, **pairs, w=(w_hbm, w_out), grid=(grid_hbm, grid_out))
    table = jnp.concatenate([b[...] for b in blocks], axis=0) * 0.5
    width, rest = table.shape[0], hot0.shape[1]
    for which, hot in enumerate((hot0, hot1, hot2)):
        held(f"c{which}"), held(f"d{which}")
        for at in range(0, base_ref.shape[1], BLOCK):
            cut = slice(at, at + BLOCK)
            column = col_ref[which, cut, :]
            base_ref[which, cut, :] = mm(pick_matrix(column, width), table) + share_ref[which, cut, :].astype(F32)
            hot[cut, :] = pick_matrix(column, rest, width)
    held("w"), held("grid")


def decode_kernel(*refs):
    *blocks, base_ref, hot0, hot1, hot2, w_ref, grid_ref, out_hbm, out_ref, out_sems = refs
    count = blocks[0].shape[0]
    table = [blocks[RIDING - 1][:count, :]] + [b[b.shape[0] - count:, :] for b in blocks]
    table = jnp.concatenate(table, axis=0) * 0.5
    step = out_ref.shape[0] // out_sems.shape[0]
    sent = []
    for at in range(0, out_ref.shape[0], step):
        cut = slice(at, at + step)
        hidden = None
        for which, hot in enumerate((hot0, hot1, hot2)):
            more = half_silu(base_ref[which, cut, :] + mm(hot[cut, :], table))
            hidden = more if hidden is None else hidden + more
        update = scaled(mm(hidden.astype(BF), w_ref[...]))
        out_ref[cut, :] = (grid_ref[cut, :].astype(F32) + update).astype(BF)
        sent.append(pltpu.make_async_copy(out_ref.at[cut, :], out_hbm.at[cut, :], out_sems.at[at // step]))
        sent[-1].start()
    for copy in sent:
        copy.wait()


def call(kernel, name, out, specs, args, scratch=(), flops=0, limit=24, outs=None, copies=0, wait=True):
    if scratch and wait:
        scratch = list(scratch) + [pltpu.SemaphoreType.DMA((16,))]
    if copies:
        scratch.append(pltpu.SemaphoreType.DMA((copies,)))
    args = [pltpu.with_memory_space_constraint(a, pltpu.HBM) if s is HB else a for s, a in zip(specs, args)]
    return pl.pallas_call(
        kernel,
        out_shape=out,
        in_specs=specs,
        out_specs=jax.tree.map(lambda _: VM, out) if outs is None else outs,
        scratch_shapes=scratch,
        compiler_params=pltpu.CompilerParams(vmem_limit_bytes=limit * MIB),
        cost_estimate=pl.CostEstimate(flops=flops, bytes_accessed=4 * MIB, transcendentals=0),
        name=name,
    )(*args)


def strip_shift(value, by):
    length = lax.axis_size("grid")
    pairs = [(i, i + by) for i in range(length) if 0 <= i + by < length]
    return lax.ppermute(value, "grid", pairs)


def exchange(blocks, steps=None):
    length = lax.axis_size("mesh")
    moved = []
    for dz, block in zip(steps or range(length), blocks):
        pairs = [(i, (i + dz) % length) for i in range(length)]
        moved.append(lax.ppermute(block, "mesh", pairs) if dz else block)
    return moved


def shards(
    grid_latent,
    mesh_latent,
    enc_source,
    enc_slot,
    enc_geometry,
    edge_count,
    slot_row,
    halo_rows,
    proc_source,
    proc_target,
    proc_geometry,
    return_rows,
    dec_source,
    dec_geometry,
    enc_weights,
    enc_lift,
    proc_weights,
    proc_lift,
    dec_weights,
    dec_lift,
):
    nodes, width = grid_latent.shape
    mesh_rows = mesh_latent.shape[0]
    n_mesh = lax.axis_size("mesh")
    count = slot_row.shape[3]
    edges, links = enc_source.shape[0], proc_source.shape[0]
    near_of = dec_source.shape[1]
    shape = jax.ShapeDtypeStruct
    block = shape((count, width), BF)
    row = shape((mesh_rows, width), BF)
    wide_row = shape((mesh_rows, width), F32)
    weight = shape((width, width), BF)
    square = pltpu.VMEM((width, width), BF)
    lifts = pltpu.VMEM(enc_lift.shape, F32)
    above = strip_shift(slot_row[0], -1)
    message, slot, *far = call(
        encode_kernel, "encode", (shape((edges, width), BF), shape((1, edges), jnp.int32)) + (block,) * n_mesh, [SM] + [HB] * 6,
        (edge_count, grid_latent, enc_source.reshape(-1, 128), enc_slot.reshape(-1, 128), enc_geometry, enc_weights, enc_lift),
        [pltpu.VMEM((nodes, width), BF), pltpu.VMEM((edges // 128, 128), jnp.int32),
         pltpu.VMEM((edges // 128, 128), jnp.int32), pltpu.VMEM((4, edges), F32), square, square, lifts,
         pltpu.VMEM((nodes, width), BF)],
        flops=5 * 10**9,
    )
    far = exchange(far)
    halo = halo_rows[0].T
    sends = pltpu.HBM((halo.size, width), BF)
    sending = pltpu.VMEM((halo.size, width), BF)
    hot = shape((halo.size, -(-mesh_rows // 128) * 128), BF)
    near = call(near_kernel, "near", (block,) * n_mesh, [VM] * 2, (message, slot), flops=10**9)
    up = call(far_kernel, "far", (row,), [VM] * (n_mesh + 1) + [ANY], (*far, above, near[0]), flops=10**8)
    near = exchange(near)
    start, own, wb, wc, wn, hot, hot_far = call(
        prep_kernel, "prep", (row, wide_row, weight, weight, weight, hot, pltpu.HBM(hot.shape, BF)),
        [ANY] + [HB] * 4, (up[0], halo, mesh_latent, enc_weights, proc_weights),
        [pltpu.VMEM(halo.shape, jnp.int32), square, square], flops=PREP, outs=(VM,) * 6 + (HB,), copies=1,
    )
    up = strip_shift(up[0], 1)
    latent, sender, sent = call(
        first_kernel, "first", (row, row, sends), [VM] * (n_mesh + 8),
        (*near, up, slot_row[0], start, own, wb, wc, wn, hot), [sending], flops=10**9, outs=(VM, VM, HB), copies=4, wait=False,
    )
    layers = proc_weights.shape[0]
    moved = shape((mesh_rows + EXTRA, width), BF)
    half = shape((links // 2, width), BF)
    index = shape((links // 128, 128), jnp.int32)
    for layer in range(layers):
        came = lax.all_to_all(
            sent.reshape(lax.axis_size("grid") * n_mesh, -1, width), ("grid", "mesh"), split_axis=0, concat_axis=0, tiled=True
        ).reshape(sent.shape)
        last = layer + 1 == layers
        operands = [
            latent, sender, proc_source.reshape(-1, 128), proc_target.reshape(-1, 128), proc_geometry, proc_lift, proc_weights,
        ]
        outs = (row, index, index, half, half) + (pltpu.HBM(weight.shape, BF),) * 2
        out_specs = (VM,) * 5 + (HB,) * 2
        scratch = [pltpu.VMEM((4, links), F32), lifts, square, square, square, square]
        specs = [VM] * 2 + [HB] * 5
        if last:
            operands += [grid_latent, dec_geometry.transpose(1, 0, 2), dec_lift, dec_weights, dec_source.T, return_rows[0]]
            specs += [HB] * 5 + [VM]
            outs = (pltpu.HBM((nodes, width), BF),) * near_of + (
                pltpu.HBM(weight.shape, BF), pltpu.HBM((near_of, nodes, 128), jnp.int16), pltpu.HBM((n_mesh * count, 128), jnp.int16),
            ) + outs
            out_specs = (HB,) * (near_of + 3) + out_specs
            scratch = [
                pltpu.VMEM((nodes, width), BF), pltpu.VMEM((near_of, 4, nodes), F32), lifts, square, square,
                pltpu.VMEM((nodes, width), F32), pltpu.VMEM((near_of, nodes, width), BF), pltpu.VMEM((near_of, nodes), jnp.int32),
                pltpu.VMEM((near_of, nodes, 128), jnp.int16), pltpu.VMEM((n_mesh * count, 128), jnp.int16),
            ] + scratch
        held = list(call(
            functools.partial(before_kernel, layer=layer, last=last), "before", outs, specs, operands, scratch, flops=10**9,
            outs=out_specs, copies=4 + 2 * near_of,
        ))
        if last:
            *shares, dec_out, places_out, rows_out = held[:near_of + 3]
            held = held[near_of + 3:]
        out = call(
            functools.partial(layer_kernel, layer=layer, last=last), "layer",
            (row, moved) + (block,) * n_mesh if last else (row, row, sends), [VM] * 7 + [HB] * 5 + [VM],
            (latent, came, *held, proc_weights, dec_weights if last else proc_weights, rows_out if last else hot_far, return_rows[0]),
            [pltpu.VMEM((links, width), BF)] + [square] * 4
            + [pltpu.VMEM((n_mesh * count, 128), jnp.int16) if last else pltpu.VMEM(hot.shape, BF), sending], flops=4 * 10**9,
            outs=(VM,) * (2 + n_mesh) if last else (VM, VM, HB), copies=4,
        )
        if last:
            latent, proj, *back = out
        else:
            latent, sender, sent = out
    proj = strip_shift(proj, -1)
    riding = back.pop(RIDING)
    back = exchange(back, (0, 1, 2))
    ahead = call(
        spread_kernel, "spread", tuple(shape((2 * count if dz == RIDING else count, width), BF) for dz in range(n_mesh)), [VM] * 2,
        (proj, riding), flops=10**8,
    )
    ahead = exchange(ahead)
    base, *hots, dec_out, rows = call(
        decode_near_kernel, "decode_near",
        (shape((near_of, nodes, width), F32),) + (shape((nodes, n_mesh * count), BF),) * near_of + (weight, shape((nodes, width), BF)),
        [VM] * n_mesh + [HB] * (near_of + 3), (*back, ahead.pop(0), *shares, places_out, dec_out, grid_latent),
        [pltpu.VMEM((near_of, nodes, 128), jnp.int16), pltpu.VMEM((near_of, nodes, width), BF)], flops=3 * 10**9,
    )
    grid_out = call(
        decode_kernel, "decode", pltpu.HBM(grid_latent.shape, BF), [VM] * (n_mesh + 5),
        (*ahead, base, *hots, dec_out, rows),
        [pltpu.VMEM((nodes, width), BF)],
        flops=3 * 10**9, outs=HB, copies=4, wait=False,
    )
    return (grid_out, latent)


def solution(mesh):
    placed = (
        P(("grid", "mesh"), None),
        P(("grid", "mesh"), None),
        P(("grid", "mesh")),
        P(("grid", "mesh")),
        P(None, ("grid", "mesh")),
        P(("grid", "mesh")),
        P(("grid", "mesh"), None, None, None),
        P(("grid", "mesh"), None, None),
        P(("grid", "mesh")),
        P(("grid", "mesh")),
        P(None, ("grid", "mesh")),
        P(("grid", "mesh"), None, None, None),
        P(("grid", "mesh"), None),
        P(None, None, ("grid", "mesh")),
        P(),
        P(),
        P(),
        P(),
        P(),
        P(),
    )
    return jax.shard_map(
        shards,
        mesh=mesh,
        in_specs=placed,
        out_specs=(P(("grid", "mesh"), None), P(("grid", "mesh"), None)),
        check_vma=False,
    )
```

```python
import functools

import jax
import jax.numpy as jnp
from jax import lax
from jax.experimental import pallas as pl
from jax.experimental.pallas import tpu as pltpu
from jax.sharding import PartitionSpec as P

BF = jnp.bfloat16
F32 = jnp.float32
VM = pl.BlockSpec(memory_space=pltpu.VMEM)
SM = pl.BlockSpec(memory_space=pltpu.SMEM)
HB = pl.BlockSpec(memory_space=pltpu.HBM)
ANY = pl.BlockSpec(memory_space=pl.ANY)
MIB = 1024 * 1024
BLOCK = 512
RIDING = 3
EXTRA = 16
PREP = 10**10


def mm(a, b):
    return lax.dot_general(a, b, (((1,), (0,)), ((), ())), preferred_element_type=F32)


def mm_tn(a, b):
    return lax.dot_general(a, b, (((0,), (0,)), ((), ())), preferred_element_type=F32)


def to_columns(row):
    n = row.shape[1]
    parts = [jnp.broadcast_to(row[:, at:at + 128], (128, 128)).T for at in range(0, n, 128)]
    return jnp.concatenate(parts, axis=0) if len(parts) > 1 else parts[0]


def lane_hits(columns, at):
    return columns == lax.broadcasted_iota(jnp.int16, columns.shape, 1) + jnp.int16(at)


def as_ones(hits):
    return jnp.where(hits, jnp.ones(hits.shape, BF), jnp.zeros(hits.shape, BF))


def pick_matrix(columns, width, start=0):
    col = columns.astype(jnp.int16)
    return jnp.concatenate([as_ones(lane_hits(col, at)) for at in range(start, start + width, 128)], axis=1)


def add_matrix(row, height):
    n = row.shape[1]
    wide = jnp.broadcast_to(row, (16, n)).astype(jnp.int16)
    wide = jnp.broadcast_to(wide[None], (height // 16, 16, n)).reshape(height, n)
    return as_ones(wide == lax.broadcasted_iota(jnp.int16, (height, n), 0))


def split3(x):
    a = x.astype(BF).astype(F32)
    r = x - a
    b = r.astype(BF).astype(F32)
    return a, b, r - b


def lift(geometry, right):
    a, b, c = split3(geometry)
    return mm_tn(jnp.concatenate([a, a, b, b, a, c], axis=0).astype(BF), right)


def lift_right(weight):
    a, b, c = split3(weight)
    return jnp.concatenate([a, b, a, b, c, a], axis=0).astype(BF)


def half_silu(half):
    return half + half * jnp.tanh(half)


def centered(weight):
    wide = weight.astype(F32)
    return (wide - jnp.mean(wide, axis=-1, keepdims=True)).astype(BF)


def scaled(v):
    return v * lax.rsqrt(jnp.mean(v * v, axis=-1, keepdims=True) + 1e-05)


def norm(v):
    c = v - jnp.mean(v, axis=-1, keepdims=True)
    return c * lax.rsqrt(jnp.mean(c * c, axis=-1, keepdims=True) + 1e-05)


def node_update(latent, own, total, w_total, w_out):
    inner = own + mm(total.astype(BF), w_total)
    hidden = half_silu(inner * 0.5).astype(BF)
    return (latent.astype(F32) + scaled(mm(hidden, w_out))).astype(BF)


def padded(table, rows):
    return jnp.concatenate([table, jnp.zeros((rows - table.shape[0], table.shape[1]), BF)], axis=0)


def pick_rows(row, table):
    wide = -(-table.shape[0] // 128) * 128
    return mm(pick_matrix(to_columns(row), wide), padded(table, wide)).astype(BF)


def lanes(ref, at, count):
    return jnp.concatenate([ref[r:r + 1, :] for r in range(at // 128, (at + count) // 128)], axis=1)


class Held:
    def __init__(self, sems, **pairs):
        self.copies, self.refs = {}, {}
        for at, (name, (src, dst)) in enumerate(pairs.items()):
            self.refs[name] = dst
            self.copies[name] = pltpu.make_async_copy(src, dst, sems.at[at])
            self.copies[name].start()

    def __call__(self, name):
        if name in self.copies:
            self.copies.pop(name).wait()
        return self.refs[name]

    def wait(self):
        for name in list(self.copies):
            self(name)


class Sent:
    def __init__(self, sems):
        self.sems, self.copies = sems, []

    def __call__(self, src, dst):
        self.copies.append(pltpu.make_async_copy(src, dst, self.sems.at[len(self.copies)]))
        self.copies[-1].start()

    def wait(self):
        for copy in self.copies:
            copy.wait()


def turned(index, count, me):
    return lax.bitwise_and(index - me, count - 1)


def row_of(rows, at):
    out = None
    for s in range(rows.shape[0]):
        part = jnp.where(at == s, rows[s:s + 1, :], 0)
        out = part if out is None else out + part
    return out


def rows_from(rows, me):
    count = rows.shape[0]
    return jnp.concatenate([row_of(rows, lax.bitwise_and(me - dz, count - 1)) for dz in range(count)], axis=1)


def rows_to(rows, me):
    count = rows.shape[0]
    return jnp.concatenate([row_of(rows, lax.bitwise_and(me + dz, count - 1)) for dz in range(count)], axis=1)


def slot_sums(slot, part, n_mesh, message, outs):
    count = outs[0].shape[0]
    band = n_mesh * count
    me = lax.axis_index("mesh")
    local = slot - part * band
    turn = turned(lax.div(local, count), n_mesh, me) * count + lax.bitwise_and(local, count - 1)
    turn = jnp.where((local >= 0) & (local < band), turn, -1)
    total = mm(add_matrix(turn, band), message)
    for dz in range(n_mesh):
        outs[dz][...] = total[dz * count:(dz + 1) * count].astype(BF)


def encode_kernel(count_ref, grid_hbm, src_hbm, slot_hbm, geo_hbm, w_hbm, lift_hbm, message_ref, slot_out, *rest):
    outs, (grid_ref, src_ref, slot_ref, geo_ref, w0_ref, w1_ref, lift_ref, table_ref, sems) = rest[:4], rest[4:]
    nodes, edges = grid_ref.shape[0], message_ref.shape[0]
    held = Held(
        sems, grid=(grid_hbm, grid_ref), w0=(w_hbm.at[0], w0_ref), src=(src_hbm, src_ref), geo=(geo_hbm, geo_ref),
        lift=(lift_hbm, lift_ref), w1=(w_hbm.at[1], w1_ref), slot=(slot_hbm, slot_ref),
    )
    held.wait()
    table_ref[...] = (mm(grid_ref[...], w0_ref[...]) * 0.5).astype(BF)
    right = lift_right(lift_ref[...] * 0.5)
    cuts = [slice(at, at + BLOCK) for at in range(0, edges, BLOCK)]
    hidden = None
    for i in range(len(cuts) + 1):
        ahead = hidden
        if i < len(cuts):
            picks = pick_matrix(to_columns(lanes(src_ref, cuts[i].start, BLOCK)), nodes)
            hidden = half_silu(mm(picks, table_ref[...]) + lift(geo_ref[:, cuts[i]], right)).astype(BF)
        if i > 0:
            message_ref[cuts[i - 1], :] = norm(mm(ahead, w1_ref[...])).astype(BF)
    slot = lanes(slot_ref, 0, edges)
    slot = jnp.where(lax.broadcasted_iota(jnp.int32, slot.shape, 1) < count_ref[0], slot, -1)
    slot_out[...] = slot
    slot_sums(slot, 1, len(outs), message_ref[...], outs)


def near_kernel(message_ref, slot_ref, *outs):
    slot_sums(slot_ref[...], 0, len(outs), message_ref[...], outs)


def prep_kernel(_, rows_ref, halo_hbm, latent_hbm, w_hbm, next_hbm, *rest):
    latent_out, own_ref, wb_out, wc_out, wn_out, hot_ref, adds_ref, hot_hbm, halo_ref, wa_ref, wc_ref, sems, out_sems = rest
    held = Held(
        sems, halo=(halo_hbm, halo_ref), latent=(latent_hbm, latent_out), wa=(w_hbm.at[2], wa_ref), wc=(w_hbm.at[4], wc_ref),
        wb=(w_hbm.at[3], wb_out), wn=(next_hbm.at[0, 0], wn_out),
    )
    adds_ref[...] = add_matrix(rows_from(rows_ref[0], lax.axis_index("mesh")), adds_ref.shape[0])
    halo = held("halo")[...].astype(F32).astype(BF)
    places, owners = halo.shape
    row = lax.broadcasted_iota(jnp.int32, (places * owners, 128), 0)
    lane = lax.broadcasted_iota(jnp.int32, row.shape, 1)
    owner = jnp.where(lax.div(row, places) == lane, 1.0, 0.0).astype(BF)
    each = lax.dot_general(owner, halo, (((1,), (1,)), ((), ())), preferred_element_type=F32)
    mine = jnp.where(lax.bitwise_and(row, places - 1)[:, :places] == lane[:, :places], each, 0.0)
    column = jnp.broadcast_to(jnp.sum(mine, axis=1, keepdims=True), row.shape).astype(jnp.int32)
    hot_ref[...] = pick_matrix(column, hot_ref.shape[1])
    sent = Sent(out_sems)
    sent(hot_ref, hot_hbm)
    own_ref[...] = mm(held("latent")[...], held("wa")[...])
    wc_out[...] = centered(held("wc")[...])
    held("wb"), held("wn")
    sent.wait()


def far_kernel(*refs):
    *blocks, rows_ref, _, out_ref = refs
    rows = rows_from(rows_ref[1], lax.axis_index("mesh"))
    table = jnp.concatenate([b[...] for b in blocks], axis=0)
    out_ref[...] = mm(add_matrix(rows, out_ref.shape[0]), table).astype(BF)


def send_rows(hot_ref, table, sent_ref, sent_hbm, sems):
    table = padded(table, hot_ref.shape[1])
    sent = Sent(sems)
    step = sent_ref.shape[0] // sems.shape[0]
    for at in range(0, sent_ref.shape[0], step):
        cut = slice(at, at + step)
        sent_ref[cut, :] = mm(hot_ref[cut, :], table).astype(BF)
        sent(sent_ref.at[cut, :], sent_hbm.at[cut, :])
    sent.wait()


def first_kernel(*refs):
    *blocks, far_ref, adds_ref, latent_ref, own_ref, wb_ref, wc_ref, wn_ref, hot_ref, out_ref, sender_ref, sent_hbm, sent_ref, out_sems = refs
    table = jnp.concatenate([b[...] for b in blocks], axis=0)
    total = mm(adds_ref[...], table)
    total = total + far_ref[...].astype(F32)
    latent = node_update(latent_ref[...], own_ref[...], total, wb_ref[...], wc_ref[...])
    out_ref[...] = latent
    sender = (mm(latent, wn_ref[...]) * 0.5).astype(BF)
    sender_ref[...] = sender
    send_rows(hot_ref, sender, sent_ref, sent_hbm, out_sems)


def before_kernel(latent_ref, sender_ref, src_hbm, tgt_hbm, geo_hbm, lift_hbm, w_hbm, *rest, layer, last):
    if last:
        (grid_hbm, decgeo_hbm, declift_hbm, dec_hbm, decsrc_hbm, rows_ref), rest = rest[:6], rest[6:]
        (*shares, decw_out, deccol_out, rowcol_out), rest = rest[:6], rest[6:]
    own_ref, src_ref, tgt_ref, *bases = rest[:5]
    (wc_out, wf_out), rest = rest[5:7], rest[7:]
    if last:
        (grid_ref, decgeo_ref, declift_ref, decv_ref, decw_ref, total_ref, share_ref, decsrc_ref, deccol_ref, rowcol_ref), rest = rest[:10], rest[10:]
    geo_ref, lift_ref, wb_ref, wd_ref, wc_ref, wf_ref, sems, out_sems = rest
    more = {}
    if last:
        more = dict(
            grid=(grid_hbm, grid_ref), decgeo=(decgeo_hbm, decgeo_ref), declift=(declift_hbm, declift_ref),
            decv=(dec_hbm.at[1], decv_ref), decw=(dec_hbm.at[2], decw_ref), decsrc=(decsrc_hbm, decsrc_ref),
        )
    held = Held(
        sems, wb=(w_hbm.at[layer, 1], wb_ref), src=(src_hbm, src_ref), tgt=(tgt_hbm, tgt_ref), geo=(geo_hbm, geo_ref),
        lift=(lift_hbm.at[layer], lift_ref), wd=(w_hbm.at[layer, 3], wd_ref), wc=(w_hbm.at[layer, 2], wc_ref),
        wf=(w_hbm.at[layer, 5], wf_ref), **more,
    )
    sent = Sent(out_sems)
    latent = latent_ref[...]
    rows = latent.shape[0]
    target = (mm(latent, held("wb")[...]) * 0.5).astype(BF)
    wide = -(-2 * rows // 128) * 128
    table = padded(jnp.concatenate([sender_ref[...], target], axis=0), wide)
    held("src"), held("tgt"), held("geo")
    right = lift_right(held("lift")[...] * 0.5)
    for part, base_ref in enumerate(bases):
        for at in range(0, base_ref.shape[0], 128):
            near = part * base_ref.shape[0] + at
            src = to_columns(lanes(src_ref, near, 128))
            src_col = jnp.where(src < rows, src, -1).astype(jnp.int16)
            tgt_col = to_columns(lanes(tgt_ref, near, 128) + rows).astype(jnp.int16)
            groups = [as_ones(lane_hits(src_col, lane) | lane_hits(tgt_col, lane)) for lane in range(0, wide, 128)]
            base = mm(jnp.concatenate(groups, axis=1), table) + lift(geo_ref[:, near:near + 128], right)
            base_ref[at:at + 128, :] = base.astype(BF)
    own_ref[...] = mm(latent, held("wd")[...]).astype(BF)
    wc_ref[...] = centered(held("wc")[...])
    sent(wc_ref, wc_out)
    wf_ref[...] = centered(held("wf")[...])
    sent(wf_ref, wf_out)
    if last:
        right = lift_right(held("declift")[...] * 0.5)
        total_ref[...] = mm(held("grid")[...], held("decv")[...]) * 0.5
        decw_ref[...] = centered(held("decw")[...])
        sent(decw_ref, decw_out)
        n_mesh, count = rows_ref.shape[1:]
        rowcol_ref[...] = to_columns(rows_to(rows_ref[0], lax.axis_index("mesh"))).astype(jnp.int16)
        sent(rowcol_ref, rowcol_out)
        held("decsrc")
        for which in range(decsrc_ref.shape[0]):
            deccol_ref[which] = place_columns(decsrc_ref[which:which + 1, :], n_mesh, count).astype(jnp.int16)
            sent(deccol_ref.at[which], deccol_out.at[which])
        held("decgeo")
        for which, out in enumerate(shares):
            for at in range(0, out.shape[0], 256):
                cut = slice(at, at + 256)
                share_ref[which, cut, :] = (lift(decgeo_ref[which, :, cut], right) + total_ref[cut, :]).astype(BF)
            sent(share_ref.at[which], out)
    sent.wait()


def layer_kernel(latent_ref, came_ref, own_ref, src_ref, tgt_ref, *rest, layer, last):
    (*bases, wc_hbm, wf_hbm, w_hbm, next_hbm, pick_ref, places_ref), rest = rest[:8], rest[8:]
    outs, (message_ref, wc_ref, we_ref, wf_ref, wn_ref, hot_ref, sent_ref, sems, out_sems) = rest[:-9], rest[-9:]
    held = Held(
        sems, wc=(wc_hbm, wc_ref), we=(w_hbm.at[layer, 4], we_ref), wf=(wf_hbm, wf_ref),
        wn=(next_hbm.at[0] if last else next_hbm.at[layer + 1, 0], wn_ref), **({} if last else dict(hot=(pick_ref, hot_ref))),
    )
    rows = latent_ref.shape[0]
    for part, base_ref in enumerate(bases):
        count = base_ref.shape[0]
        cut = slice(part * count, (part + 1) * count)
        columns = to_columns(lanes(src_ref, part * count, count)) - rows
        half = mm(pick_matrix(columns, came_ref.shape[0]), came_ref[...]) + base_ref[...].astype(F32)
        message_ref[cut, :] = scaled(mm(half_silu(half).astype(BF), held("wc")[...])).astype(BF)
    total = mm(add_matrix(lanes(tgt_ref, 0, message_ref.shape[0]), rows), message_ref[...])
    latent = node_update(latent_ref[...], own_ref[...].astype(F32), total, held("we")[...], held("wf")[...])
    outs[0][...] = latent
    onward = mm(latent, held("wn")[...])
    if last:
        onward = onward.astype(BF)
        outs[1][:rows, :] = onward
        places = jnp.concatenate([places_ref[1, m:m + 1, :] for m in range(places_ref.shape[1])], axis=1).astype(F32)
        outs[1][rows:, :] = jnp.broadcast_to(places, (outs[1].shape[0] - rows, places.shape[1])).astype(BF)
        spread(to_columns(rows_to(places_ref[0], lax.axis_index("mesh"))), onward, outs[2:])
    else:
        onward = (onward * 0.5).astype(BF)
        outs[1][...] = onward
        send_rows(held("hot"), onward, sent_ref, outs[2], out_sems)


def spread(columns, table, outs):
    wide = -(-table.shape[0] // 128) * 128
    picked = mm(pick_matrix(columns, wide), padded(table, wide)).astype(BF)
    count = outs[0].shape[0]
    for dz, out in enumerate(outs):
        out[out.shape[0] - count:, :] = picked[dz * count:(dz + 1) * count]


def spread_kernel(moved_ref, riding_ref, *outs):
    rows = moved_ref.shape[0] - EXTRA
    count = outs[0].shape[0]
    places = moved_ref[rows:rows + 16, :].astype(F32).astype(jnp.int32)[:1, :]
    places = jnp.concatenate([places[:, m * count:(m + 1) * count] for m in range(len(outs))], axis=0)
    outs[RIDING][:count, :] = riding_ref[...]
    spread(to_columns(rows_to(places, lax.axis_index("mesh"))), moved_ref[:rows, :], outs)


def place_columns(place, n_mesh, count):
    me = lax.axis_index("mesh")
    block = lax.div(place, count)
    turn = lax.bitwise_and(me - block, n_mesh - 1) + lax.bitwise_and(block, -n_mesh)
    turn = jnp.where(turn == RIDING, n_mesh, jnp.where((turn > RIDING) & (turn <= n_mesh), turn - 1, turn))
    return to_columns(turn * count + lax.bitwise_and(place, count - 1))


def decode_near_kernel(*refs):
    *blocks, dec0, dec1, dec2, col_hbm, w_hbm, grid_hbm, base_ref, hot0, hot1, hot2, w_out, grid_out, col_ref, share_ref, sems = refs
    pairs = {}
    for i, dec in enumerate((dec0, dec1, dec2)):
        pairs.update({f"c{i}": (col_hbm.at[i], col_ref.at[i]), f"d{i}": (dec, share_ref.at[i])})
    held = Held(sems, **pairs, w=(w_hbm, w_out), grid=(grid_hbm, grid_out))
    table = jnp.concatenate([b[...] for b in blocks], axis=0) * 0.5
    width, rest = table.shape[0], hot0.shape[1]
    for which, hot in enumerate((hot0, hot1, hot2)):
        held(f"c{which}"), held(f"d{which}")
        for at in range(0, base_ref.shape[1], BLOCK):
            cut = slice(at, at + BLOCK)
            column = col_ref[which, cut, :]
            base_ref[which, cut, :] = mm(pick_matrix(column, width), table) + share_ref[which, cut, :].astype(F32)
            hot[cut, :] = pick_matrix(column, rest, width)
    held("w"), held("grid")


def decode_kernel(*refs):
    *blocks, base_ref, hot0, hot1, hot2, w_ref, grid_ref, out_hbm, out_ref, out_sems = refs
    count = blocks[0].shape[0]
    table = [blocks[RIDING - 1][:count, :]] + [b[b.shape[0] - count:, :] for b in blocks]
    table = jnp.concatenate(table, axis=0) * 0.5
    step = out_ref.shape[0] // out_sems.shape[0]
    sent = []
    for at in range(0, out_ref.shape[0], step):
        cut = slice(at, at + step)
        hidden = None
        for which, hot in enumerate((hot0, hot1, hot2)):
            more = half_silu(base_ref[which, cut, :] + mm(hot[cut, :], table))
            hidden = more if hidden is None else hidden + more
        update = scaled(mm(hidden.astype(BF), w_ref[...]))
        out_ref[cut, :] = (grid_ref[cut, :].astype(F32) + update).astype(BF)
        sent.append(pltpu.make_async_copy(out_ref.at[cut, :], out_hbm.at[cut, :], out_sems.at[at // step]))
        sent[-1].start()
    for copy in sent:
        copy.wait()


def call(kernel, name, out, specs, args, scratch=(), flops=0, limit=24, outs=None, copies=0, wait=True):
    if scratch and wait:
        scratch = list(scratch) + [pltpu.SemaphoreType.DMA((16,))]
    if copies:
        scratch.append(pltpu.SemaphoreType.DMA((copies,)))
    args = [pltpu.with_memory_space_constraint(a, pltpu.HBM) if s is HB else a for s, a in zip(specs, args)]
    return pl.pallas_call(
        kernel,
        out_shape=out,
        in_specs=specs,
        out_specs=jax.tree.map(lambda _: VM, out) if outs is None else outs,
        scratch_shapes=scratch,
        compiler_params=pltpu.CompilerParams(vmem_limit_bytes=limit * MIB),
        cost_estimate=pl.CostEstimate(flops=flops, bytes_accessed=4 * MIB, transcendentals=0),
        name=name,
    )(*args)


def strip_shift(value, by):
    length = lax.axis_size("grid")
    pairs = [(i, i + by) for i in range(length) if 0 <= i + by < length]
    return lax.ppermute(value, "grid", pairs)


def exchange(blocks, steps=None):
    length = lax.axis_size("mesh")
    moved = []
    for dz, block in zip(steps or range(length), blocks):
        pairs = [(i, (i + dz) % length) for i in range(length)]
        moved.append(lax.ppermute(block, "mesh", pairs) if dz else block)
    return moved


def shards(
    grid_latent,
    mesh_latent,
    enc_source,
    enc_slot,
    enc_geometry,
    edge_count,
    slot_row,
    halo_rows,
    proc_source,
    proc_target,
    proc_geometry,
    return_rows,
    dec_source,
    dec_geometry,
    enc_weights,
    enc_lift,
    proc_weights,
    proc_lift,
    dec_weights,
    dec_lift,
):
    nodes, width = grid_latent.shape
    mesh_rows = mesh_latent.shape[0]
    n_mesh = lax.axis_size("mesh")
    count = slot_row.shape[3]
    edges, links = enc_source.shape[0], proc_source.shape[0]
    near_of = dec_source.shape[1]
    shape = jax.ShapeDtypeStruct
    block = shape((count, width), BF)
    row = shape((mesh_rows, width), BF)
    wide_row = shape((mesh_rows, width), F32)
    weight = shape((width, width), BF)
    square = pltpu.VMEM((width, width), BF)
    lifts = pltpu.VMEM(enc_lift.shape, F32)
    above = strip_shift(slot_row[0], -1)
    message, slot, *far = call(
        encode_kernel, "encode", (shape((edges, width), BF), shape((1, edges), jnp.int32)) + (block,) * n_mesh, [SM] + [HB] * 6,
        (edge_count, grid_latent, enc_source.reshape(-1, 128), enc_slot.reshape(-1, 128), enc_geometry, enc_weights, enc_lift),
        [pltpu.VMEM((nodes, width), BF), pltpu.VMEM((edges // 128, 128), jnp.int32),
         pltpu.VMEM((edges // 128, 128), jnp.int32), pltpu.VMEM((4, edges), F32), square, square, lifts,
         pltpu.VMEM((nodes, width), BF)],
        flops=5 * 10**9,
    )
    far = exchange(far)
    halo = halo_rows[0].T
    sends = pltpu.HBM((halo.size, width), BF)
    sending = pltpu.VMEM((halo.size, width), BF)
    hot = shape((halo.size, -(-mesh_rows // 128) * 128), BF)
    near = call(near_kernel, "near", (block,) * n_mesh, [VM] * 2, (message, slot), flops=10**9)
    up = call(far_kernel, "far", (row,), [VM] * (n_mesh + 1) + [ANY], (*far, above, near[0]), flops=10**8)
    near = exchange(near)
    start, own, wb, wc, wn, hot, adds, hot_far = call(
        prep_kernel, "prep", (row, wide_row, weight, weight, weight, hot, shape((mesh_rows, n_mesh * count), BF), pltpu.HBM(hot.shape, BF)),
        [ANY, VM] + [HB] * 4, (up[0], slot_row[0], halo, mesh_latent, enc_weights, proc_weights),
        [pltpu.VMEM(halo.shape, jnp.int32), square, square], flops=PREP, outs=(VM,) * 7 + (HB,), copies=1,
    )
    up = strip_shift(up[0], 1)
    latent, sender, sent = call(
        first_kernel, "first", (row, row, sends), [VM] * (n_mesh + 8),
        (*near, up, adds, start, own, wb, wc, wn, hot), [sending], flops=10**9, outs=(VM, VM, HB), copies=4, wait=False,
    )
    layers = proc_weights.shape[0]
    moved = shape((mesh_rows + EXTRA, width), BF)
    half = shape((links // 2, width), BF)
    index = shape((links // 128, 128), jnp.int32)
    for layer in range(layers):
        came = lax.all_to_all(
            sent.reshape(lax.axis_size("grid") * n_mesh, -1, width), ("grid", "mesh"), split_axis=0, concat_axis=0, tiled=True
        ).reshape(sent.shape)
        last = layer + 1 == layers
        operands = [
            latent, sender, proc_source.reshape(-1, 128), proc_target.reshape(-1, 128), proc_geometry, proc_lift, proc_weights,
        ]
        outs = (row, index, index, half, half) + (pltpu.HBM(weight.shape, BF),) * 2
        out_specs = (VM,) * 5 + (HB,) * 2
        scratch = [pltpu.VMEM((4, links), F32), lifts, square, square, square, square]
        specs = [VM] * 2 + [HB] * 5
        if last:
            operands += [grid_latent, dec_geometry.transpose(1, 0, 2), dec_lift, dec_weights, dec_source.T, return_rows[0]]
            specs += [HB] * 5 + [VM]
            outs = (pltpu.HBM((nodes, width), BF),) * near_of + (
                pltpu.HBM(weight.shape, BF), pltpu.HBM((near_of, nodes, 128), jnp.int16), pltpu.HBM((n_mesh * count, 128), jnp.int16),
            ) + outs
            out_specs = (HB,) * (near_of + 3) + out_specs
            scratch = [
                pltpu.VMEM((nodes, width), BF), pltpu.VMEM((near_of, 4, nodes), F32), lifts, square, square,
                pltpu.VMEM((nodes, width), F32), pltpu.VMEM((near_of, nodes, width), BF), pltpu.VMEM((near_of, nodes), jnp.int32),
                pltpu.VMEM((near_of, nodes, 128), jnp.int16), pltpu.VMEM((n_mesh * count, 128), jnp.int16),
            ] + scratch
        held = list(call(
            functools.partial(before_kernel, layer=layer, last=last), "before", outs, specs, operands, scratch, flops=10**9,
            outs=out_specs, copies=4 + 2 * near_of,
        ))
        if last:
            *shares, dec_out, places_out, rows_out = held[:near_of + 3]
            held = held[near_of + 3:]
        out = call(
            functools.partial(layer_kernel, layer=layer, last=last), "layer",
            (row, moved) + (block,) * n_mesh if last else (row, row, sends), [VM] * 7 + [HB] * 5 + [VM],
            (latent, came, *held, proc_weights, dec_weights if last else proc_weights, rows_out if last else hot_far, return_rows[0]),
            [pltpu.VMEM((links, width), BF)] + [square] * 4
            + [pltpu.VMEM((n_mesh * count, 128), jnp.int16) if last else pltpu.VMEM(hot.shape, BF), sending], flops=4 * 10**9,
            outs=(VM,) * (2 + n_mesh) if last else (VM, VM, HB), copies=4,
        )
        if last:
            latent, proj, *back = out
        else:
            latent, sender, sent = out
    proj = strip_shift(proj, -1)
    riding = back.pop(RIDING)
    back = exchange(back, (0, 1, 2))
    ahead = call(
        spread_kernel, "spread", tuple(shape((2 * count if dz == RIDING else count, width), BF) for dz in range(n_mesh)), [VM] * 2,
        (proj, riding), flops=10**8,
    )
    ahead = exchange(ahead)
    base, *hots, dec_out, rows = call(
        decode_near_kernel, "decode_near",
        (shape((near_of, nodes, width), F32),) + (shape((nodes, n_mesh * count), BF),) * near_of + (weight, shape((nodes, width), BF)),
        [VM] * n_mesh + [HB] * (near_of + 3), (*back, ahead.pop(0), *shares, places_out, dec_out, grid_latent),
        [pltpu.VMEM((near_of, nodes, 128), jnp.int16), pltpu.VMEM((near_of, nodes, width), BF)], flops=3 * 10**9,
    )
    grid_out = call(
        decode_kernel, "decode", pltpu.HBM(grid_latent.shape, BF), [VM] * (n_mesh + 5),
        (*ahead, base, *hots, dec_out, rows),
        [pltpu.VMEM((nodes, width), BF)],
        flops=3 * 10**9, outs=HB, copies=4, wait=False,
    )
    return (grid_out, latent)


def solution(mesh):
    placed = (
        P(("grid", "mesh"), None),
        P(("grid", "mesh"), None),
        P(("grid", "mesh")),
        P(("grid", "mesh")),
        P(None, ("grid", "mesh")),
        P(("grid", "mesh")),
        P(("grid", "mesh"), None, None, None),
        P(("grid", "mesh"), None, None),
        P(("grid", "mesh")),
        P(("grid", "mesh")),
        P(None, ("grid", "mesh")),
        P(("grid", "mesh"), None, None, None),
        P(("grid", "mesh"), None),
        P(None, None, ("grid", "mesh")),
        P(),
        P(),
        P(),
        P(),
        P(),
        P(),
    )
    return jax.shard_map(
        shards,
        mesh=mesh,
        in_specs=placed,
        out_specs=(P(("grid", "mesh"), None), P(("grid", "mesh"), None)),
        check_vma=False,
    )
```
